256 devices in a mesh: pipe: 8 (over x, core), ctx: 32 (over y, z).
Axes of the slice: x: 4, y: 4, z: 8, core: 2. Of those that a mesh axis runs over, the one named last changes fastest.
Arguments:
- queries: bfloat16 [8, 4096, 4096], P('pipe', 'ctx'), may hold values from -60 to 60
- key_projection: bfloat16 [8, 4096, 512], P('pipe', 'ctx'), may hold values from -6 to 6
- value_projection: bfloat16 [8, 4096, 512], P('pipe', 'ctx'), may hold values from -6 to 6
- forward_out: bfloat16 [8, 4096, 4096], P('pipe', 'ctx'), may hold values from -6 to 6
- incoming: bfloat16 [8, 4096, 4096], P('pipe', 'ctx'), may hold values from -6 to 6
- doc_lengths: int32 [8, 16], P('pipe'), may hold values from 1 to 1024, 4096 in all within a row
- pair_of: int32 [8, 32], P('pipe'), may hold values from 0 to 31, each once within a row
Outputs:
- query_grad: bfloat16 [8, 4096, 4096], P('pipe', 'ctx')
- key_gradient: bfloat16 [8, 4096, 512], P('pipe', 'ctx')
- value_gradient: bfloat16 [8, 4096, 512], P('pipe', 'ctx')
The draws below stay inside these ranges and needn't reach their ends.
All inputs are finite; a program needn't handle non-finite values.
Results may differ from the reference program's by a relative error of at most 0.005.
Values may be sent and summed in bfloat16 or wider, within the bound.
No kernel may reach another device: no remote copies, remote signals or barrier semaphores. Data moves between devices by JAX's collectives and lax.ppermute only.
A program may use at most 128 MiB of HBM per device.

```python
import math
import jax
import jax.numpy as jnp
import numpy as np
from jax import lax

QUERY_HEADS = 32
KEY_VALUE_HEADS = 4
HEAD_SIZE = 128
TOK_DEV = 128
DOCS = 16
BATCH_TOKENS = 4096
RELAY_SECTIONS = 8
N_CTX = 32


def hidden_parts(key):
    key_layout = (RELAY_SECTIONS, BATCH_TOKENS, KEY_VALUE_HEADS * HEAD_SIZE)
    shared_keys = jax.random.normal(jax.random.fold_in(key, 11), key_layout, jnp.float32)
    shared_keys = jnp.clip(shared_keys, -6.0, 6.0)
    return shared_keys


def draw_key_projection(key, part):
    return hidden_parts(key).astype(jnp.bfloat16)


def draw_queries(key, part):
    query_layout = (RELAY_SECTIONS, BATCH_TOKENS, QUERY_HEADS * HEAD_SIZE)
    return jnp.clip(jax.random.normal(jax.random.fold_in(key, 22), query_layout, jnp.float32), -6.0, 6.0).astype(jnp.bfloat16)


def shard_levels(key, extent, pieces, least, high):
    gain = 1.0
    for axis_at, blocks in pieces:
        heights = jax.random.uniform(jax.random.fold_in(jax.random.fold_in(key, 6), axis_at), (blocks,), jnp.float32, least / len(pieces), high / len(pieces))
        gain = gain * jnp.repeat(jnp.exp(heights), extent[axis_at] // blocks).reshape((-1,) + (1,) * (len(extent) - 1 - axis_at))
    return gain


def length_profile(amount, total, bound, skew):
    loads = [(1 << 20) // math.isqrt(rank ** skew) + 1 for rank in range(2, amount + 1)]
    surplus, counts = total - bound - (amount - 1), [1] * (amount - 1)
    while surplus > 0:
        free = [i for i in range(amount - 1) if counts[i] < bound]
        mass, remaining = sum([loads[i] for i in free]), surplus
        for i in free:
            more = min(bound - counts[i], max(1, remaining * loads[i] // mass), surplus)
            counts[i] = counts[i] + more
            surplus = surplus - more
    return np.array([bound] + counts)


def ragged_sizes(rng, count, total, reach, lean):
    if count == 2:
        one = jax.random.randint(rng, (), max(1, total - reach), min(reach, total - 1) + 1)
        return jnp.stack([one, total - one])
    tallies = jnp.asarray(length_profile(count, total, reach, lean), jnp.int32)
    couples = (count - 1) // 2
    source_of, receiver = tallies[1:1 + 2 * couples:2], tallies[2:2 + 2 * couples:2]
    slack = jnp.minimum(source_of - 1, reach - receiver)
    shifted = jax.random.randint(jax.random.fold_in(rng, 1), (couples,), 0, 1 << 20) % (slack + 1)
    tallies = tallies.at[1:1 + 2 * couples:2].set(source_of - shifted).at[2:2 + 2 * couples:2].set(receiver + shifted)
    return tallies[jax.random.permutation(jax.random.fold_in(rng, 2), count)]


def bell_draw(stream_key, extent, width, reach, split=(), kind=jnp.bfloat16):
    factor_of = shard_levels(stream_key, extent, split, -0.22, 0.18) if split else 1.0
    values = jax.random.normal(stream_key, extent, jnp.float32) * width * factor_of
    return jnp.minimum(jnp.maximum(values, -reach), reach).astype(kind)


def setup_inputs(seed: int = 0) -> dict:
    key_of = jax.random.split(jax.random.key(seed), 8)
    return {
        "queries": draw_queries(jax.random.fold_in(key_of[7], 71), 0),
        "key_projection": draw_key_projection(jax.random.fold_in(key_of[7], 71), 0),
        "value_projection": bell_draw(key_of[2], (RELAY_SECTIONS, BATCH_TOKENS, KEY_VALUE_HEADS * HEAD_SIZE), 1.0, 6.0, ((0, 8), (1, 32))),
        "forward_out": bell_draw(key_of[3], (RELAY_SECTIONS, BATCH_TOKENS, QUERY_HEADS * HEAD_SIZE), 1.0, 6.0, ((0, 8), (1, 32))),
        "incoming": bell_draw(key_of[4], (RELAY_SECTIONS, BATCH_TOKENS, QUERY_HEADS * HEAD_SIZE), 1.0, 6.0, ((0, 8), (1, 32))),
        "doc_lengths": jax.vmap(lambda own: ragged_sizes(own, DOCS, BATCH_TOKENS, BATCH_TOKENS // 4, 2))(jax.random.split(key_of[5], RELAY_SECTIONS)).reshape((RELAY_SECTIONS, DOCS)).astype(jnp.int32),
        "pair_of": jax.vmap(lambda own: jax.random.permutation(own, N_CTX))(jax.random.split(key_of[6], RELAY_SECTIONS)).reshape((RELAY_SECTIONS, N_CTX)).astype(jnp.int32),
    }


def slot_positions(pair_ids, slot_rows):
    device_count = pair_ids.shape[0]
    slot_blocks = jnp.stack([pair_ids, 2 * device_count - 1 - pair_ids], axis=1).reshape(-1)
    offsets = jnp.arange(slot_rows, dtype=jnp.int32)
    return (slot_blocks[:, None] * slot_rows + offsets[None, :]).reshape(-1).astype(jnp.int32)

def doc_starts(lengths_row, positions):
    doc_ends = jnp.cumsum(lengths_row)
    before = doc_ends[None, :] <= positions[:, None]
    return lax.optimization_barrier(jnp.sum(jnp.where(before, lengths_row[None, :], 0), axis=1)).astype(jnp.int32)

def heads_leading(block_of_rows, head_count):
    count_of_rows = block_of_rows.shape[0]
    return block_of_rows.reshape(count_of_rows, head_count, -1).transpose(1, 0, 2)

def one_section(section_args):
    queries, key_projection, value_projection, forward_out, out_grad, lengths_row, pair_ids = section_args
    query_group_size = QUERY_HEADS // KEY_VALUE_HEADS
    score_scale = 1.0 / math.sqrt(HEAD_SIZE)
    count_of_rows = queries.shape[0]
    positions = slot_positions(pair_ids.astype(jnp.int32), TOK_DEV // 2)
    starts = doc_starts(lengths_row.astype(jnp.int32), positions)
    keep_mask = (positions[None, :] <= positions[:, None]) & (positions[None, :] >= starts[:, None])
    query_heads = heads_leading(queries, QUERY_HEADS)
    heads_of_keys = jnp.repeat(heads_leading(key_projection, KEY_VALUE_HEADS), query_group_size, axis=0)
    heads_of_values = jnp.repeat(heads_leading(value_projection, KEY_VALUE_HEADS), query_group_size, axis=0)
    grad_heads = heads_leading(out_grad, QUERY_HEADS)
    output_heads = heads_leading(forward_out, QUERY_HEADS)

    def per_head(head_args):
        query_rows, key_rows, value_rows, grad_rows, output_rows = head_args
        scores = score_scale * jnp.dot(query_rows, key_rows.T, preferred_element_type=jnp.float32)
        scores = jnp.where(keep_mask, scores, -jnp.inf)
        row_peak = lax.optimization_barrier(jnp.max(scores, axis=1, keepdims=True))
        log_total = row_peak + jnp.log(lax.optimization_barrier(jnp.sum(jnp.exp(scores - row_peak), axis=1, keepdims=True)))
        prob_rows = jnp.where(keep_mask, jnp.exp(scores - log_total), 0.0)
        row_delta = lax.optimization_barrier(jnp.sum(grad_rows.astype(jnp.float32) * output_rows.astype(jnp.float32), axis=1, keepdims=True))
        dprobs = jnp.dot(grad_rows, value_rows.T, preferred_element_type=jnp.float32)
        dscores = (prob_rows * (dprobs - row_delta)).astype(jnp.bfloat16)
        prob_low = prob_rows.astype(jnp.bfloat16)
        query_part = score_scale * jnp.dot(dscores, key_rows, preferred_element_type=jnp.float32)
        key_portion = score_scale * jnp.dot(dscores.T, query_rows, preferred_element_type=jnp.float32)
        value_portion = jnp.dot(prob_low.T, grad_rows, preferred_element_type=jnp.float32)
        return (query_part, key_portion, value_portion)
    query_part, key_portion, value_portion = lax.map(per_head, (query_heads, heads_of_keys, heads_of_values, grad_heads, output_heads))
    query_grad = query_part.transpose(1, 0, 2).reshape(count_of_rows, QUERY_HEADS * HEAD_SIZE).astype(jnp.bfloat16)
    key_gradient = lax.optimization_barrier(jnp.sum(key_portion.reshape(KEY_VALUE_HEADS, query_group_size, count_of_rows, HEAD_SIZE), axis=1))
    key_gradient = key_gradient.transpose(1, 0, 2).reshape(count_of_rows, KEY_VALUE_HEADS * HEAD_SIZE).astype(jnp.bfloat16)
    value_gradient = lax.optimization_barrier(jnp.sum(value_portion.reshape(KEY_VALUE_HEADS, query_group_size, count_of_rows, HEAD_SIZE), axis=1))
    value_gradient = value_gradient.transpose(1, 0, 2).reshape(count_of_rows, KEY_VALUE_HEADS * HEAD_SIZE).astype(jnp.bfloat16)
    return (query_grad, key_gradient, value_gradient)

def reference(queries, key_projection, value_projection, forward_out, incoming, doc_lengths, pair_of):
    out_grad = jnp.roll(incoming, -1, axis=0)
    query_grad, key_gradient, value_gradient = lax.map(one_section, (queries, key_projection, value_projection, forward_out, out_grad, doc_lengths, pair_of))
    return (query_grad, key_gradient, value_gradient)
```

```python
import functools
import math

import jax
import jax.numpy as jnp
from jax import lax
from jax.experimental import pallas as pl
from jax.experimental.pallas import tpu as pltpu
from jax.sharding import PartitionSpec as P

HEADS = 4
GROUP = 8
DIM = 128
TOK = 128
SLOT = 64
ROWS = GROUP * SLOT
DOCS = 16
NY = 4
NZ = 8
SECTIONS = 8
ALL = TOK * NY * NZ
BLOCKS = 2 * NY
TILE = 256
WINDOW = 1024
MAX_TILES = (WINDOW + SLOT - 2) // TILE + 2
SCALE = 1.0 / math.sqrt(DIM)
LOG2E = 1.4426950408889634
LOW = -1e30
WIDE = GROUP * DIM

NT = (((1,), (1,)), ((), ()))
NN = (((1,), (0,)), ((), ()))


def along_y(x, by):
    return lax.ppermute(
        x, "ctx", [(c, (c // NZ + by) % NY * NZ + c % NZ) for c in range(NY * NZ)]
    )


def along_pipe_y(x, by):
    count = NY * NZ
    return lax.ppermute(
        x,
        ("pipe", "ctx"),
        [
            (p * count + c, (p - 1) % SECTIONS * count + (c // NZ + by) % NY * NZ + c % NZ)
            for p in range(SECTIONS)
            for c in range(count)
        ],
    )


def dot(a, b, dims):
    return lax.dot_general(a, b, dims, preferred_element_type=jnp.float32)


def whole(count):
    return [pl.BlockSpec(memory_space=pltpu.VMEM)] * count


def scalars():
    return pl.BlockSpec(memory_space=pltpu.SMEM)


def params(mib):
    return pltpu.CompilerParams(vmem_limit_bytes=mib << 20)


def column(y, k, width):
    return pl.ds(pl.multiple_of(lax.rem(y + k, NY) * width, width), width)


def pack_kv_body(info, key, value, *outs):
    for k in range(NY):
        outs[k][:, :DIM] = key[:, column(info[48], k, DIM)]
        outs[k][:, DIM:] = value[:, column(info[48], k, DIM)]


def pack_kv(info, key, value):
    return pl.pallas_call(
        pack_kv_body,
        out_shape=[jax.ShapeDtypeStruct((TOK, 2 * DIM), jnp.bfloat16)] * NY,
        in_specs=[scalars()] + whole(2),
        out_specs=whole(NY),
        name="pack_kv",
    )(info, key, value)


def pack_wide_body(info, x, *outs):
    for k in range(NY):
        outs[k][...] = x[:, column(info[48], k, WIDE)]


def pack_wide(info, x):
    return pl.pallas_call(
        pack_wide_body,
        out_shape=[jax.ShapeDtypeStruct((TOK, WIDE), jnp.bfloat16)] * NY,
        in_specs=[scalars()] + whole(1),
        out_specs=whole(NY),
        name="pack_wide",
    )(info, x)


def delta_body(info, grad, out, *outs):
    ones = jnp.ones((8, DIM), jnp.bfloat16)
    for k in range(NY):
        columns = column(info[48], k, WIDE)
        product = grad[:, columns].astype(jnp.float32) * out[:, columns].astype(jnp.float32)
        high = product.astype(jnp.bfloat16)
        low = (product - high.astype(jnp.float32)).astype(jnp.bfloat16)
        for s in range(2):
            rows = slice(s * SLOT, (s + 1) * SLOT)
            parts = []
            for part in (high, low):
                stacked = jnp.concatenate(
                    [part[rows, h * DIM : (h + 1) * DIM] for h in range(GROUP)], axis=0
                )
                parts.append(dot(ones, stacked, NT))
            outs[k][s * 8 : (s + 1) * 8, :] = parts[0] + parts[1]


def row_deltas(info, grad, out):
    return pl.pallas_call(
        delta_body,
        out_shape=[jax.ShapeDtypeStruct((16, ROWS), jnp.float32)] * NY,
        in_specs=[scalars()] + whole(2),
        out_specs=whole(NY),
        name="row_deltas",
    )(info, grad, out)


def main_body(info, *refs):
    queries, grads, deltas = refs[0:NY], refs[NY : 2 * NY], refs[2 * NY : 3 * NY]
    gathered = refs[3 * NY]
    query_outs = refs[3 * NY + 1 : 4 * NY + 1]
    kv_out = refs[4 * NY + 1]
    (keys, values, keys_t, key_acc, value_acc, scores, query_acc, q_rows, g_rows, d_rows, dq_rows) = refs[
        4 * NY + 2 :
    ]
    y, z = info[48], info[49]

    def block_at(zi, yr, s):
        pid = info[lax.rem(y + NY - yr, NY) * NZ + zi]
        return jnp.where(s == 0, pid, 2 * NY * NZ - 1 - pid)

    def sort_in(zi, carry):
        for yr in range(NY):
            for s in range(2):
                dst = pl.ds(pl.multiple_of(block_at(zi, yr, s) * SLOT, SLOT), SLOT)
                src = pl.ds(pl.multiple_of(zi * (NY * TOK) + yr * TOK + s * SLOT, SLOT), SLOT)
                keys[dst, :] = gathered[src, :DIM]
                values[dst, :] = gathered[src, DIM:]
        return carry

    lax.fori_loop(0, NZ, sort_in, 0)

    for t in range(ALL // TILE):
        keys_t[t] = keys[t * TILE : (t + 1) * TILE, :].T
    key_acc[...] = jnp.zeros_like(key_acc)
    value_acc[...] = jnp.zeros_like(value_acc)

    for yr in range(NY):
        for s in range(2):
            rows = slice(s * SLOT, (s + 1) * SLOT)
            for h in range(GROUP):
                at = slice(h * SLOT, (h + 1) * SLOT)
                q_rows[2 * yr + s, at, :] = queries[yr][rows, h * DIM : (h + 1) * DIM]
                g_rows[2 * yr + s, at, :] = grads[yr][rows, h * DIM : (h + 1) * DIM]
            d_rows[2 * yr + s] = deltas[yr][s * 8 : (s + 1) * 8, :]

    def start_of(pos):
        start = jnp.zeros_like(pos)
        for i in range(DOCS):
            end = info[32 + i]
            start = jnp.where(end <= pos, end, start)
        return start

    def block_step(i, carry):
        qb = q_rows[i]
        gb = g_rows[i]
        first = block_at(z, i // 2, lax.rem(i, 2)) * SLOT
        lane = lax.broadcasted_iota(jnp.int32, (1, ROWS), 1)
        q_pos = first + (lane & (SLOT - 1))
        q_start = start_of(q_pos)
        low_tile = start_of(first) // TILE
        high_tile = (first + SLOT - 1) // TILE + 1

        def score_step(t, peak):
            kt = keys[pl.ds(pl.multiple_of(t * TILE, TILE), TILE), :]
            st = dot(kt, qb, NT)
            k_pos = t * TILE + lax.broadcasted_iota(jnp.int32, (TILE, ROWS), 0)
            st = jnp.where((k_pos <= q_pos) & (k_pos >= q_start), st, LOW)
            scores[t - low_tile] = st
            return jnp.maximum(peak, jnp.max(st.reshape(TILE // 8, 8, ROWS), axis=0))

        peak = lax.fori_loop(
            low_tile, high_tile, score_step, jnp.full((8, ROWS), LOW, jnp.float32)
        )
        peak = jnp.max(peak, axis=0, keepdims=True)

        def exp_step(t, total):
            e = jnp.exp2((scores[t - low_tile] - peak) * (SCALE * LOG2E))
            scores[t - low_tile] = e
            return total + jnp.sum(e.reshape(TILE // 8, 8, ROWS), axis=0)

        total = lax.fori_loop(low_tile, high_tile, exp_step, jnp.zeros((8, ROWS), jnp.float32))
        inverse = 1.0 / jnp.sum(total, axis=0, keepdims=True)
        delta = d_rows[i][0:1, :]
        query_acc[...] = jnp.zeros_like(query_acc)

        def grad_step(t, carry):
            rows = pl.ds(pl.multiple_of(t * TILE, TILE), TILE)
            prob = scores[t - low_tile] * inverse
            dprob = dot(values[rows, :], gb, NT)
            dscore = (prob * (dprob - delta)).astype(jnp.bfloat16)
            key_acc[rows, :] += dot(dscore, qb, NN)
            value_acc[rows, :] += dot(prob.astype(jnp.bfloat16), gb, NN)
            query_acc[...] += dot(keys_t[t], dscore, NN)
            return carry

        lax.fori_loop(low_tile, high_tile, grad_step, 0)
        dq_rows[i] = (query_acc[...].T * SCALE).astype(jnp.bfloat16)
        return carry

    lax.fori_loop(0, BLOCKS, block_step, 0)

    for yr in range(NY):
        for s in range(2):
            for h in range(GROUP):
                query_outs[yr][s * SLOT : (s + 1) * SLOT, h * DIM : (h + 1) * DIM] = dq_rows[
                    2 * yr + s, h * SLOT : (h + 1) * SLOT, :
                ]

    def sort_out(zi, carry):
        for yr in range(NY):
            for s in range(2):
                src = pl.ds(pl.multiple_of(block_at(zi, yr, s) * SLOT, SLOT), SLOT)
                dst = pl.ds(pl.multiple_of(zi * (NY * TOK) + yr * TOK + s * SLOT, SLOT), SLOT)
                kv_out[dst, :DIM] = (key_acc[src, :] * SCALE).astype(kv_out.dtype)
                kv_out[dst, DIM:] = value_acc[src, :].astype(kv_out.dtype)
        return carry

    lax.fori_loop(0, NZ, sort_out, 0)


def attention_grads(info, queries, grads, deltas, gathered):
    bf16, f32 = jnp.bfloat16, jnp.float32
    return pl.pallas_call(
        main_body,
        out_shape=[jax.ShapeDtypeStruct((TOK, WIDE), bf16)] * NY
        + [jax.ShapeDtypeStruct((ALL, 2 * DIM), bf16)],
        in_specs=[scalars()] + whole(3 * NY + 1),
        out_specs=whole(NY + 1),
        scratch_shapes=[
            pltpu.VMEM((ALL, DIM), bf16),
            pltpu.VMEM((ALL, DIM), bf16),
            pltpu.VMEM((ALL // TILE, DIM, TILE), bf16),
            pltpu.VMEM((ALL, DIM), f32),
            pltpu.VMEM((ALL, DIM), f32),
            pltpu.VMEM((MAX_TILES, TILE, ROWS), f32),
            pltpu.VMEM((DIM, ROWS), f32),
            pltpu.VMEM((BLOCKS, ROWS, DIM), bf16),
            pltpu.VMEM((BLOCKS, ROWS, DIM), bf16),
            pltpu.VMEM((BLOCKS, 8, ROWS), f32),
            pltpu.VMEM((BLOCKS, ROWS, DIM), bf16),
        ],
        compiler_params=params(48),
        name="attention_grads",
    )(info, *queries, *grads, *deltas, gathered)


def place_wide_body(info, *refs):
    for k in range(NY):
        refs[NY][:, column(info[48], k, WIDE)] = refs[k][...]


def place_wide(info, pieces):
    return pl.pallas_call(
        place_wide_body,
        out_shape=jax.ShapeDtypeStruct((TOK, HEADS * WIDE), jnp.bfloat16),
        in_specs=[scalars()] + whole(NY),
        out_specs=pl.BlockSpec(memory_space=pltpu.VMEM),
        name="place_wide",
    )(info, *pieces)


def place_kv_body(info, *refs):
    for k in range(NY):
        refs[NY][:, column(info[48], k, DIM)] = refs[k][:, :DIM]
        refs[NY + 1][:, column(info[48], k, DIM)] = refs[k][:, DIM:]


def place_kv(info, pieces):
    return pl.pallas_call(
        place_kv_body,
        out_shape=[jax.ShapeDtypeStruct((TOK, HEADS * DIM), jnp.bfloat16)] * 2,
        in_specs=[scalars()] + whole(NY),
        out_specs=whole(2),
        name="place_kv",
    )(info, *pieces)


def per_device(
    queries, key_projection, value_projection, forward_out, incoming, doc_lengths, pair_of
):
    place = lax.axis_index("ctx").astype(jnp.int32)
    info = jnp.concatenate(
        [
            pair_of[0].astype(jnp.int32),
            jnp.cumsum(doc_lengths[0]).astype(jnp.int32),
            jnp.stack([place // NZ, place % NZ]),
        ]
    )
    columns_of_ring = [[y * NZ + z for z in range(NZ)] for y in range(NY)]

    def to_heads(pieces, move):
        return [pieces[0]] + [move(pieces[k], k) for k in range(1, NY)]

    with jax.named_scope("keys_values_in"):
        kv = to_heads(pack_kv(info, key_projection[0], value_projection[0]), along_y)
        kv = jnp.concatenate(kv, axis=0)
        gathered = lax.all_gather(
            kv, "ctx", axis=0, tiled=True, axis_index_groups=columns_of_ring
        )
    with jax.named_scope("queries_in"):
        query_pieces = to_heads(pack_wide(info, queries[0]), along_y)
    with jax.named_scope("grads_in"):
        grad_pieces = [along_pipe_y(x, k) for k, x in enumerate(pack_wide(info, incoming[0]))]
    with jax.named_scope("deltas_in"):
        next_out = lax.ppermute(
            forward_out[0], "pipe", [(p, (p + 1) % SECTIONS) for p in range(SECTIONS)]
        )
        delta_pieces = [
            along_pipe_y(x, k) for k, x in enumerate(row_deltas(info, incoming[0], next_out))
        ]
    *query_parts, kv_part = attention_grads(
        info, query_pieces, grad_pieces, delta_pieces, gathered
    )
    with jax.named_scope("query_grads_out"):
        query_grad = place_wide(info, to_heads(query_parts, lambda x, k: along_y(x, -k)))
    with jax.named_scope("key_value_grads_out"):
        kv_sum = lax.psum_scatter(
            kv_part, "ctx", scatter_dimension=0, tiled=True, axis_index_groups=columns_of_ring
        )
        kv_pieces = [kv_sum[k * TOK : (k + 1) * TOK] for k in range(NY)]
        key_gradient, value_gradient = place_kv(
            info, to_heads(kv_pieces, lambda x, k: along_y(x, -k))
        )
    return query_grad[None], key_gradient[None], value_gradient[None]


def solution(mesh):
    tokens = P("pipe", "ctx", None)
    return jax.shard_map(
        per_device,
        mesh=mesh,
        in_specs=(tokens,) * 5 + (P("pipe", None),) * 2,
        out_specs=(tokens,) * 3,
        check_vma=False,
    )
```

```python
import functools
import math

import jax
import jax.numpy as jnp
from jax import lax
from jax.experimental import pallas as pl
from jax.experimental.pallas import tpu as pltpu
from jax.sharding import PartitionSpec as P

HEADS = 4
GROUP = 8
DIM = 128
TOK = 128
SLOT = 64
ROWS = GROUP * SLOT
DOCS = 16
NY = 4
NZ = 8
SECTIONS = 8
ALL = TOK * NY * NZ
BLOCKS = 2 * NY
TILE = 256
PACE = 2
QUERY_STEP = 2
GRAD_STEP = 3
BACK_STEP = 3
WINDOW = 1024
MAX_TILES = 5
MAX_VISITS = 48
VISITS = 64
VISIT_BLOCK = 80
VISIT_TILE = VISIT_BLOCK + MAX_VISITS
VISIT_SLOT = VISIT_TILE + MAX_VISITS
VISIT_FIRST = VISIT_SLOT + MAX_VISITS
PLAN_SIZE = VISIT_FIRST + MAX_VISITS
SCALE = 1.0 / math.sqrt(DIM)
LOG2E = 1.4426950408889634
LOW = -1e30
WIDE = GROUP * DIM
EXTRA = 32
GRAD_ROWS = 2 * ROWS + 2 * (ROWS // DIM) * (EXTRA // 2)
OFFSETS = tuple(range(-(NZ // 2), NZ // 2))

NT = (((1,), (1,)), ((), ()))
NN = (((1,), (0,)), ((), ()))


def along_y(x, by):
    return lax.ppermute(
        x, "ctx", [(c, (c // NZ + by) % NY * NZ + c % NZ) for c in range(NY * NZ)]
    )


def along_z(x, by):
    return lax.ppermute(
        x, "ctx", [(c, c // NZ * NZ + (c % NZ + by) % NZ) for c in range(NY * NZ)]
    )


def together(*arrays):
    return lax.optimization_barrier(arrays)


def gather_z(x, query_pieces, packed, send):
    right = left = x
    pieces = {0: x}
    for step in range(1, NZ // 2 + 1):
        right = along_z(right, 1)
        if step < NZ // 2:
            left = along_z(left, -1)
            held = [right, left]
            if step == 1:
                held += packed
            if step == QUERY_STEP:
                held += query_pieces
            if step == GRAD_STEP:
                held += grad_pieces
            right, left, *held = together(*held)
            if step == 1:
                plan, grad_pieces = held[:2], send(held[2 : 2 + NY])
                held = held[2 + NY :]
            if step == QUERY_STEP:
                query_pieces, held = held[:NY], held[NY:]
            if step == GRAD_STEP:
                grad_pieces = held
            pieces[step] = left
        pieces[-step] = right
    return [pieces[off] for off in OFFSETS], query_pieces, plan, grad_pieces


def add_low(moving, own):
    return (moving.astype(jnp.float32) + own).astype(jnp.bfloat16)


def sum_z(parts, queries):
    parts = dict(zip(OFFSETS, parts))
    half = NZ // 2
    left, right = parts[-half], parts[half - 1]
    for step in range(1, half + 1):
        left = along_z(left, -1)
        if step < half:
            right = along_z(right, 1)
            if step == BACK_STEP:
                left, right, *queries = together(left, right, *queries)
            else:
                left, right = together(left, right)
            left = add_low(left, parts[step - half])
            if step < half - 1:
                right = add_low(right, parts[half - 1 - step])
    total = parts[0] + left.astype(jnp.float32) + right.astype(jnp.float32)
    return total.astype(jnp.bfloat16), queries


def dot(a, b, dims):
    return lax.dot_general(a, b, dims, preferred_element_type=jnp.float32)


def whole(count):
    return [pl.BlockSpec(memory_space=pltpu.VMEM)] * count


def scalars():
    return pl.BlockSpec(memory_space=pltpu.SMEM)


def params(mib):
    return pltpu.CompilerParams(vmem_limit_bytes=mib << 20)


def own_y():
    return lax.axis_index("ctx") // NZ


def column(y, k, width):
    return pl.ds(pl.multiple_of(lax.rem(y + k, NY) * width, width), width)


def pack_kv_body(key, value, *outs):
    y = own_y()
    for k in range(NY):
        outs[k][:, :DIM] = key[:, column(y, k, DIM)]
        outs[k][:, DIM:] = value[:, column(y, k, DIM)]


def pack_kv(key, value):
    return pl.pallas_call(
        pack_kv_body,
        out_shape=[jax.ShapeDtypeStruct((TOK, 2 * DIM), jnp.bfloat16)] * NY,
        in_specs=whole(2),
        out_specs=whole(NY),
        name="pack_kv",
    )(key, value)


def stacked(piece, s):
    rows = slice(s * SLOT, (s + 1) * SLOT)
    return jnp.concatenate([piece[rows, h * DIM : (h + 1) * DIM] for h in range(GROUP)], axis=0)


def pack_queries_body(x, *outs):
    y = own_y()
    for k in range(NY):
        piece = x[:, column(y, k, WIDE)]
        for s in range(2):
            outs[k][s * ROWS : (s + 1) * ROWS, :] = stacked(piece, s)


def pack_queries(x):
    return pl.pallas_call(
        pack_queries_body,
        out_shape=[jax.ShapeDtypeStruct((2 * ROWS, DIM), jnp.bfloat16)] * NY,
        in_specs=whole(1),
        out_specs=whole(NY),
        name="pack_queries",
    )(x)


def pack_grads_body(grad, out, *outs):
    y = own_y()
    ones = jnp.ones((EXTRA // 2, DIM), jnp.bfloat16)
    line = lax.broadcasted_iota(jnp.int32, (EXTRA // 2, DIM), 0)
    for k in range(NY):
        columns = column(y, k, WIDE)
        piece = grad[:, columns]
        product = piece.astype(jnp.float32) * out[:, columns].astype(jnp.float32)
        high = product.astype(jnp.bfloat16)
        low = (product - high.astype(jnp.float32)).astype(jnp.bfloat16)
        for s in range(2):
            outs[k][s * ROWS : (s + 1) * ROWS, :] = stacked(piece, s)
            delta = dot(ones, stacked(high, s), NT) + dot(ones, stacked(low, s), NT)
            for c in range(ROWS // DIM):
                part = delta[:, c * DIM : (c + 1) * DIM]
                first = part.astype(jnp.bfloat16).astype(jnp.float32)
                second = (part - first).astype(jnp.bfloat16).astype(jnp.float32)
                third = part - first - second
                coded = jnp.where(line == 0, first, jnp.where(line == 1, second, third))
                at = 2 * ROWS + (s * (ROWS // DIM) + c) * (EXTRA // 2)
                outs[k][at : at + EXTRA // 2, :] = coded.astype(jnp.bfloat16)


def pack_grads(grad, out):
    return pl.pallas_call(
        pack_grads_body,
        out_shape=[jax.ShapeDtypeStruct((GRAD_ROWS, DIM), jnp.bfloat16)] * NY,
        in_specs=whole(2),
        out_specs=whole(NY),
        name="pack_grads",
    )(grad, out)


def plan_body(pairs, lengths, plan, starts):
    own = lax.axis_index("ctx")
    y, z = own // NZ, lax.rem(own, NZ)

    def block_at(zi, yr, s):
        pid = pairs[0, lax.rem(y + NY - yr, NY) * NZ + zi]
        return pid if s == 0 else 2 * NY * NZ - 1 - pid

    for n, off in enumerate(OFFSETS):
        for yr in range(NY):
            for s in range(2):
                plan[(n * NY + yr) * 2 + s] = block_at(lax.rem(z + NZ + off, NZ), yr, s) * SLOT

    ends = []
    for i in range(DOCS):
        ends.append(lengths[0, i] + (ends[-1] if ends else 0))

    def start_of(pos):
        start = jnp.zeros_like(pos)
        for end in ends:
            start = jnp.where(end <= pos, end, start)
        return start

    lane = lax.broadcasted_iota(jnp.int32, (BLOCKS, ROWS), 1) & (SLOT - 1)
    line = lax.broadcasted_iota(jnp.int32, (BLOCKS, ROWS), 0)
    firsts = jnp.zeros((BLOCKS, ROWS), jnp.int32)
    count = jnp.int32(0)
    for i in range(BLOCKS):
        first = block_at(z, i // 2, i % 2) * SLOT
        firsts = jnp.where(line == i, first, firsts)
        low_tile = start_of(first) // TILE
        high_tile = (first + SLOT - 1) // TILE + 1

        def list_tile(t, n, i=i, first=first, low_tile=low_tile):
            plan[VISIT_BLOCK + n] = i
            plan[VISIT_TILE + n] = t
            plan[VISIT_SLOT + n] = t - low_tile
            plan[VISIT_FIRST + n] = first
            return n + 1

        count = lax.fori_loop(low_tile, high_tile, list_tile, count)
    for extra in range(PACE - 1):
        plan[VISIT_BLOCK + count + extra] = 0
        plan[VISIT_TILE + count + extra] = 0
        plan[VISIT_SLOT + count + extra] = MAX_TILES
        plan[VISIT_FIRST + count + extra] = 0
    plan[VISITS] = count
    starts[...] = start_of(firsts + lane)


def make_plan(pairs, lengths):
    return pl.pallas_call(
        plan_body,
        out_shape=[
            jax.ShapeDtypeStruct((PLAN_SIZE,), jnp.int32),
            jax.ShapeDtypeStruct((BLOCKS, ROWS), jnp.int32),
        ],
        in_specs=[scalars(), scalars()],
        out_specs=[scalars(), pl.BlockSpec(memory_space=pltpu.VMEM)],
        name="make_plan",
    )(pairs, lengths)


def main_body(plan, starts, *refs):
    queries, grads, gathered = refs[0:NY], refs[NY : 2 * NY], refs[2 * NY : 2 * NY + NZ]
    query_outs = refs[2 * NY + NZ : 3 * NY + NZ]
    kv_outs = refs[3 * NY + NZ : 3 * NY + 2 * NZ]
    keys, values, keys_t, key_acc, value_acc, scores, tops, sums, query_acc = refs[
        3 * NY + 2 * NZ : 3 * NY + 2 * NZ + 9
    ]
    q_rows, g_rows, d_rows, sems = refs[3 * NY + 2 * NZ + 9 :]

    loads = [pltpu.make_async_copy(queries[k], q_rows.at[k], sems.at[k]) for k in range(NY)]
    loads += [pltpu.make_async_copy(grads[k], g_rows.at[k], sems.at[NY + k]) for k in range(NY)]
    for load in loads:
        load.start()

    def sorted_rows(n, yr, s):
        return pl.ds(pl.multiple_of(plan[(n * NY + yr) * 2 + s], SLOT), SLOT)

    for n, piece in enumerate(gathered):
        for yr in range(NY):
            for s in range(2):
                dst = sorted_rows(n, yr, s)
                src = slice(yr * TOK + s * SLOT, yr * TOK + (s + 1) * SLOT)
                keys[dst, :] = piece[src, :DIM]
                values[dst, :] = piece[src, DIM:]

    for t in range(ALL // TILE):
        keys_t[t] = keys[t * TILE : (t + 1) * TILE, :].T
    key_acc[...] = jnp.zeros_like(key_acc)
    value_acc[...] = jnp.zeros_like(value_acc)
    query_acc[...] = jnp.zeros_like(query_acc)
    tops[...] = jnp.full_like(tops, LOW)
    sums[...] = jnp.zeros_like(sums)

    lane = lax.broadcasted_iota(jnp.int32, (1, ROWS), 1) & (SLOT - 1)
    for load in loads:
        load.wait()
    for i in range(BLOCKS):
        for c in range(ROWS // DIM):
            at = 2 * ROWS + ((i % 2) * (ROWS // DIM) + c) * (EXTRA // 2)
            coded = g_rows[i // 2, at : at + EXTRA // 2, :].astype(jnp.float32)
            d_rows[i : i + 1, c * DIM : (c + 1) * DIM] = coded[0:1] + coded[1:2] + coded[2:3]

    def place_of(v):
        i = plan[VISIT_BLOCK + v]
        return i, i // 2, pl.ds(pl.multiple_of(lax.rem(i, 2) * ROWS, ROWS), ROWS)

    def score_step(n, carry):
        raw = []
        for u in range(PACE):
            v = n * PACE + u
            i, yr, own = place_of(v)
            t = plan[VISIT_TILE + v]
            kt = keys[pl.ds(pl.multiple_of(t * TILE, TILE), TILE), :]
            raw.append(dot(kt, q_rows[yr, own, :], NT))
        for u, st in enumerate(raw):
            v = n * PACE + u
            i, slot = plan[VISIT_BLOCK + v], plan[VISIT_SLOT + v]
            k_pos = plan[VISIT_TILE + v] * TILE + lax.broadcasted_iota(jnp.int32, (TILE, ROWS), 0)
            q_pos = plan[VISIT_FIRST + v] + lane
            st = jnp.where((k_pos <= q_pos) & (k_pos >= starts[pl.ds(i, 1), :]), st, LOW)
            top = jnp.max(st, axis=0, keepdims=True)
            e = jnp.exp2((st - top) * (SCALE * LOG2E))
            scores[v] = e
            tops[slot, pl.ds(i, 1), :] = top
            sums[slot, pl.ds(i, 1), :] = jnp.sum(e, axis=0, keepdims=True)
        return carry

    steps = (plan[VISITS] + PACE - 1) // PACE
    lax.fori_loop(0, steps, score_step, 0)

    found = tops[:MAX_TILES]
    weights = jnp.exp2((found - jnp.max(found, axis=0, keepdims=True)) * (SCALE * LOG2E))
    total = jnp.sum(weights * sums[:MAX_TILES], axis=0, keepdims=True)
    tops[:MAX_TILES] = weights * (1.0 / total)
    tops[MAX_TILES] = jnp.zeros((BLOCKS, ROWS), jnp.float32)

    def grad_step(n, carry):
        low_pairs = []
        for u in range(PACE):
            v = n * PACE + u
            i, yr, own = place_of(v)
            rows = pl.ds(pl.multiple_of(plan[VISIT_TILE + v] * TILE, TILE), TILE)
            dprob = dot(values[rows, :], g_rows[yr, own, :], NT)
            prob = scores[v] * tops[plan[VISIT_SLOT + v], pl.ds(i, 1), :]
            dscore = prob * (dprob - d_rows[pl.ds(i, 1), :])
            low_pairs.append((prob.astype(jnp.bfloat16), dscore.astype(jnp.bfloat16)))
        terms = []
        for u, (prob, dscore) in enumerate(low_pairs):
            v = n * PACE + u
            i, yr, own = place_of(v)
            terms.append(
                (
                    dot(prob, g_rows[yr, own, :], NN),
                    dot(dscore, q_rows[yr, own, :], NN),
                    dot(keys_t[plan[VISIT_TILE + v]], dscore, NN),
                )
            )
        for u, (value_term, key_term, query_term) in enumerate(terms):
            v = n * PACE + u
            rows = pl.ds(pl.multiple_of(plan[VISIT_TILE + v] * TILE, TILE), TILE)
            value_acc[rows, :] += value_term
            key_acc[rows, :] += key_term
            query_acc[plan[VISIT_BLOCK + v]] += query_term
        return carry

    lax.fori_loop(0, steps, grad_step, 0)

    for i in range(BLOCKS):
        own = slice((i % 2) * ROWS, (i % 2 + 1) * ROWS)
        q_rows[i // 2, own, :] = (query_acc[i] * SCALE).astype(jnp.bfloat16).T

    stores = [
        pltpu.make_async_copy(q_rows.at[k], query_outs[k], sems.at[k]) for k in range(NY)
    ]
    for store in stores:
        store.start()
    for n, piece in enumerate(kv_outs):
        for yr in range(NY):
            for s in range(2):
                src = sorted_rows(n, yr, s)
                dst = slice(yr * TOK + s * SLOT, yr * TOK + (s + 1) * SLOT)
                piece[dst, :DIM] = (key_acc[src, :] * SCALE).astype(piece.dtype)
                piece[dst, DIM:] = value_acc[src, :].astype(piece.dtype)
    for store in stores:
        store.wait()


def attention_grads(plan, queries, grads, gathered):
    bf16, f32 = jnp.bfloat16, jnp.float32
    anywhere = pl.BlockSpec(memory_space=pl.ANY)
    return pl.pallas_call(
        main_body,
        out_shape=[jax.ShapeDtypeStruct((2 * ROWS, DIM), bf16)] * NY
        + [
            jax.ShapeDtypeStruct(
                (NY * TOK, 2 * DIM), bf16 if off in (NZ // 2 - 1, -(NZ // 2)) else f32
            )
            for off in OFFSETS
        ],
        in_specs=[scalars()] + whole(1) + [anywhere] * (2 * NY) + whole(NZ),
        out_specs=[anywhere] * NY + whole(NZ),
        scratch_shapes=[
            pltpu.VMEM((ALL, DIM), bf16),
            pltpu.VMEM((ALL, DIM), bf16),
            pltpu.VMEM((ALL // TILE, DIM, TILE), bf16),
            pltpu.VMEM((ALL, DIM), f32),
            pltpu.VMEM((ALL, DIM), f32),
            pltpu.VMEM((BLOCKS * MAX_TILES + PACE, TILE, ROWS), f32),
            pltpu.VMEM((MAX_TILES + 1, BLOCKS, ROWS), f32),
            pltpu.VMEM((MAX_TILES + 1, BLOCKS, ROWS), f32),
            pltpu.VMEM((BLOCKS, DIM, ROWS), f32),
            pltpu.VMEM((NY, 2 * ROWS, DIM), bf16),
            pltpu.VMEM((NY, GRAD_ROWS, DIM), bf16),
            pltpu.VMEM((BLOCKS, ROWS), f32),
            pltpu.SemaphoreType.DMA((2 * NY,)),
        ],
        compiler_params=params(40),
        name="attention_grads",
    )(*plan, *queries, *grads, *gathered)


def place_wide_body(*refs):
    y = own_y()
    for k in range(NY):
        start = lax.rem(y + k, NY) * WIDE
        for s in range(2):
            for h in range(GROUP):
                refs[NY][
                    s * SLOT : (s + 1) * SLOT,
                    pl.ds(pl.multiple_of(start + h * DIM, DIM), DIM),
                ] = refs[k][s * ROWS + h * SLOT : s * ROWS + (h + 1) * SLOT, :]


def place_wide(pieces):
    return pl.pallas_call(
        place_wide_body,
        out_shape=jax.ShapeDtypeStruct((TOK, HEADS * WIDE), jnp.bfloat16),
        in_specs=whole(NY),
        out_specs=pl.BlockSpec(memory_space=pltpu.VMEM),
        name="place_wide",
    )(*pieces)


def place_kv_body(*refs):
    y = own_y()
    for k in range(NY):
        refs[NY][:, column(y, k, DIM)] = refs[k][:, :DIM]
        refs[NY + 1][:, column(y, k, DIM)] = refs[k][:, DIM:]


def place_kv(pieces):
    return pl.pallas_call(
        place_kv_body,
        out_shape=[jax.ShapeDtypeStruct((TOK, HEADS * DIM), jnp.bfloat16)] * 2,
        in_specs=whole(NY),
        out_specs=whole(2),
        name="place_kv",
    )(*pieces)


def per_device(
    queries, key_projection, value_projection, forward_out, incoming, doc_lengths, pair_of
):
    def to_heads(pieces, move):
        return [pieces[0]] + [move(pieces[k], k) for k in range(1, NY)]

    with jax.named_scope("grads_shift"):
        out_grad = lax.ppermute(
            incoming[0], "pipe", [(p, (p - 1) % SECTIONS) for p in range(SECTIONS)]
        )
    with jax.named_scope("keys_values_in"):
        kv = to_heads(pack_kv(key_projection[0], value_projection[0]), along_y)
        packed_queries = pack_queries(queries[0])
        *kv, first, second, third, fourth = together(*kv, *packed_queries)
        packed_queries = [first, second, third, fourth]
        kv = jnp.concatenate(kv, axis=0)
    with jax.named_scope("queries_in"):
        query_pieces = to_heads(packed_queries, along_y)
    with jax.named_scope("plan"):
        plan = make_plan(pair_of, doc_lengths)
    with jax.named_scope("grads_pack"):
        packed_grads = pack_grads(out_grad, forward_out[0])
    with jax.named_scope("keys_values_ring"):
        gathered, query_pieces, plan, grad_pieces = gather_z(
            kv, query_pieces, [*plan, *packed_grads], lambda x: to_heads(x, along_y)
        )
    parts = attention_grads(plan, query_pieces, grad_pieces, gathered)
    query_parts, kv_parts = parts[:NY], parts[NY:]
    with jax.named_scope("query_grads_out"):
        query_parts = to_heads(query_parts, lambda x, k: along_y(x, -k))
    with jax.named_scope("key_value_grads_ring"):
        kv_sum, query_parts = sum_z(kv_parts, query_parts)
    with jax.named_scope("query_grads_place"):
        query_grad = place_wide(query_parts)
    with jax.named_scope("key_value_grads_out"):
        kv_pieces = [kv_sum[k * TOK : (k + 1) * TOK] for k in range(NY)]
        key_gradient, value_gradient = place_kv(
            to_heads(kv_pieces, lambda x, k: along_y(x, -k))
        )
    return query_grad[None], key_gradient[None], value_gradient[None]


def solution(mesh):
    tokens = P("pipe", "ctx", None)
    return jax.shard_map(
        per_device,
        mesh=mesh,
        in_specs=(tokens,) * 5 + (P("pipe", None),) * 2,
        out_specs=(tokens,) * 3,
        check_vma=False,
    )
```

```python
import functools
import math

import jax
import jax.numpy as jnp
from jax import lax
from jax.experimental import pallas as pl
from jax.experimental.pallas import tpu as pltpu
from jax.sharding import PartitionSpec as P

HEADS = 4
GROUP = 8
DIM = 128
TOK = 128
SLOT = 64
ROWS = GROUP * SLOT
DOCS = 16
NY = 4
NZ = 8
SECTIONS = 8
ALL = TOK * NY * NZ
BLOCKS = 2 * NY
TILE = 256
PACE = 4
PACK_STEP = 2
PLAN_STEP = 1
BACK_STEP = 3
WINDOW = 1024
MAX_TILES = 5
MAX_VISITS = 48
VISITS = 64
VISIT_BLOCK = 80
VISIT_TILE = VISIT_BLOCK + MAX_VISITS
VISIT_SLOT = VISIT_TILE + MAX_VISITS
VISIT_FIRST = VISIT_SLOT + MAX_VISITS
PLAN_SIZE = VISIT_FIRST + MAX_VISITS
SCALE = 1.0 / math.sqrt(DIM)
LOG2E = 1.4426950408889634
LOW = -1e30
WIDE = GROUP * DIM
EXTRA = 32
GRAD_ROWS = 2 * ROWS + 2 * (ROWS // DIM) * (EXTRA // 2)
OFFSETS = tuple(range(-(NZ // 2), NZ // 2))

NT = (((1,), (1,)), ((), ()))
NN = (((1,), (0,)), ((), ()))


def along_y(x, by):
    return lax.ppermute(
        x, "ctx", [(c, (c // NZ + by) % NY * NZ + c % NZ) for c in range(NY * NZ)]
    )


def along_z(x, by):
    return lax.ppermute(
        x, "ctx", [(c, c // NZ * NZ + (c % NZ + by) % NZ) for c in range(NY * NZ)]
    )


def together(*arrays):
    return lax.optimization_barrier(arrays)


def gather_z(x, plan, packed):
    right = left = x
    pieces = {0: x}
    for step in range(1, NZ // 2):
        right, left = along_z(right, 1), along_z(left, -1)
        if step == PLAN_STEP:
            right, left, *plan = together(right, left, *plan)
        elif step == PACK_STEP:
            right, left, *packed = together(right, left, *packed)
        else:
            right, left = together(right, left)
        pieces[-step], pieces[step] = right, left
    pieces[-(NZ // 2)] = along_z(right, 1)
    return [pieces[off] for off in OFFSETS], plan, packed


def add_low(moving, own):
    return (moving.astype(jnp.float32) + own).astype(jnp.bfloat16)


def sum_z(parts, queries):
    parts = dict(zip(OFFSETS, parts))
    half = NZ // 2
    left, right = parts[-half], parts[half - 1]
    for step in range(1, half + 1):
        left = along_z(left, -1)
        if step < half:
            right = along_z(right, 1)
            if step == BACK_STEP:
                left, right, *queries = together(left, right, *queries)
            else:
                left, right = together(left, right)
            left = add_low(left, parts[step - half])
            if step < half - 1:
                right = add_low(right, parts[half - 1 - step])
    query_grad = place_wide(queries)
    left, query_grad = together(left, query_grad)
    total = parts[0] + left.astype(jnp.float32) + right.astype(jnp.float32)
    return total.astype(jnp.bfloat16), query_grad


def dot(a, b, dims):
    return lax.dot_general(a, b, dims, preferred_element_type=jnp.float32)


def whole(count):
    return [pl.BlockSpec(memory_space=pltpu.VMEM)] * count


def scalars():
    return pl.BlockSpec(memory_space=pltpu.SMEM)


def params(mib):
    return pltpu.CompilerParams(vmem_limit_bytes=mib << 20)


def own_y():
    return lax.axis_index("ctx") // NZ


def column(y, k, width):
    return pl.ds(pl.multiple_of(lax.rem(y + k, NY) * width, width), width)


def pack_kv_body(key, value, *outs):
    y = own_y()
    for k in range(NY):
        outs[k][:, :DIM] = key[:, column(y, k, DIM)]
        outs[k][:, DIM:] = value[:, column(y, k, DIM)]


def pack_kv(key, value):
    return pl.pallas_call(
        pack_kv_body,
        out_shape=[jax.ShapeDtypeStruct((TOK, 2 * DIM), jnp.bfloat16)] * NY,
        in_specs=whole(2),
        out_specs=whole(NY),
        compiler_params=params(4),
        name="pack_kv",
    )(key, value)


def stacked(piece, s):
    rows = slice(s * SLOT, (s + 1) * SLOT)
    return jnp.concatenate([piece[rows, h * DIM : (h + 1) * DIM] for h in range(GROUP)], axis=0)


def pack_queries_body(x, *outs):
    y = own_y()
    for k in range(NY):
        piece = x[:, column(y, k, WIDE)]
        for s in range(2):
            outs[k][s * ROWS : (s + 1) * ROWS, :] = stacked(piece, s)


def pack_queries(x):
    return pl.pallas_call(
        pack_queries_body,
        out_shape=[jax.ShapeDtypeStruct((2 * ROWS, DIM), jnp.bfloat16)] * NY,
        in_specs=whole(1),
        out_specs=whole(NY),
        compiler_params=params(8),
        name="pack_queries",
    )(x)


def pack_grads_body(grad, out, *outs):
    y = own_y()
    ones = jnp.ones((EXTRA // 2, DIM), jnp.bfloat16)
    line = lax.broadcasted_iota(jnp.int32, (EXTRA // 2, DIM), 0)
    for k in range(NY):
        columns = column(y, k, WIDE)
        piece = grad[:, columns]
        product = piece.astype(jnp.float32) * out[:, columns].astype(jnp.float32)
        high = product.astype(jnp.bfloat16)
        low = (product - high.astype(jnp.float32)).astype(jnp.bfloat16)
        for s in range(2):
            outs[k][s * ROWS : (s + 1) * ROWS, :] = stacked(piece, s)
            delta = dot(ones, stacked(high, s), NT) + dot(ones, stacked(low, s), NT)
            for c in range(ROWS // DIM):
                part = delta[:, c * DIM : (c + 1) * DIM]
                first = part.astype(jnp.bfloat16).astype(jnp.float32)
                second = (part - first).astype(jnp.bfloat16).astype(jnp.float32)
                third = part - first - second
                coded = jnp.where(line == 0, first, jnp.where(line == 1, second, third))
                at = 2 * ROWS + (s * (ROWS // DIM) + c) * (EXTRA // 2)
                outs[k][at : at + EXTRA // 2, :] = coded.astype(jnp.bfloat16)


def pack_grads(grad, out):
    return pl.pallas_call(
        pack_grads_body,
        out_shape=[jax.ShapeDtypeStruct((GRAD_ROWS, DIM), jnp.bfloat16)] * NY,
        in_specs=whole(2),
        out_specs=whole(NY),
        compiler_params=params(16),
        name="pack_grads",
    )(grad, out)


def plan_body(pairs, lengths, plan, starts):
    own = lax.axis_index("ctx")
    y, z = own // NZ, lax.rem(own, NZ)

    def block_at(zi, yr, s):
        pid = pairs[0, lax.rem(y + NY - yr, NY) * NZ + zi]
        return pid if s == 0 else 2 * NY * NZ - 1 - pid

    for n, off in enumerate(OFFSETS):
        for yr in range(NY):
            for s in range(2):
                plan[(n * NY + yr) * 2 + s] = block_at(lax.rem(z + NZ + off, NZ), yr, s) * SLOT

    ends = []
    for i in range(DOCS):
        ends.append(lengths[0, i] + (ends[-1] if ends else 0))

    def start_of(pos):
        start = jnp.zeros_like(pos)
        for end in ends:
            start = jnp.where(end <= pos, end, start)
        return start

    lane = lax.broadcasted_iota(jnp.int32, (BLOCKS, ROWS), 1) & (SLOT - 1)
    line = lax.broadcasted_iota(jnp.int32, (BLOCKS, ROWS), 0)
    firsts = jnp.zeros((BLOCKS, ROWS), jnp.int32)
    count = jnp.int32(0)
    for i in range(BLOCKS):
        first = block_at(z, i // 2, i % 2) * SLOT
        firsts = jnp.where(line == i, first, firsts)
        low_tile = start_of(first) // TILE
        high_tile = (first + SLOT - 1) // TILE + 1

        def list_tile(t, n, i=i, first=first, low_tile=low_tile):
            plan[VISIT_BLOCK + n] = i
            plan[VISIT_TILE + n] = t
            plan[VISIT_SLOT + n] = t - low_tile
            plan[VISIT_FIRST + n] = first
            return n + 1

        count = lax.fori_loop(low_tile, high_tile, list_tile, count)
    for extra in range(PACE - 1):
        plan[VISIT_BLOCK + count + extra] = 0
        plan[VISIT_TILE + count + extra] = 0
        plan[VISIT_SLOT + count + extra] = MAX_TILES
        plan[VISIT_FIRST + count + extra] = 0
    plan[VISITS] = count
    starts[...] = start_of(firsts + lane)


def make_plan(pairs, lengths):
    return pl.pallas_call(
        plan_body,
        out_shape=[
            jax.ShapeDtypeStruct((PLAN_SIZE,), jnp.int32),
            jax.ShapeDtypeStruct((BLOCKS, ROWS), jnp.int32),
        ],
        in_specs=[scalars(), scalars()],
        out_specs=[scalars(), pl.BlockSpec(memory_space=pltpu.VMEM)],
        compiler_params=params(4),
        name="make_plan",
    )(pairs, lengths)


def main_body(plan, starts, *refs):
    queries, grads, gathered = refs[0:NY], refs[NY : 2 * NY], refs[2 * NY : 2 * NY + NZ]
    query_outs = refs[2 * NY + NZ : 3 * NY + NZ]
    kv_outs = refs[3 * NY + NZ : 3 * NY + 2 * NZ]
    keys, values, keys_t, key_acc, value_acc, scores, tops, sums, query_acc = refs[
        3 * NY + 2 * NZ : 3 * NY + 2 * NZ + 9
    ]
    q_rows, g_rows, d_rows, sems = refs[3 * NY + 2 * NZ + 9 :]

    loads = [pltpu.make_async_copy(queries[k], q_rows.at[k], sems.at[k]) for k in range(NY)]
    loads += [pltpu.make_async_copy(grads[k], g_rows.at[k], sems.at[NY + k]) for k in range(NY)]
    for load in loads:
        load.start()

    def sorted_rows(n, yr, s):
        return pl.ds(pl.multiple_of(plan[(n * NY + yr) * 2 + s], SLOT), SLOT)

    for n, piece in enumerate(gathered):
        for yr in range(NY):
            for s in range(2):
                dst = sorted_rows(n, yr, s)
                src = slice(yr * TOK + s * SLOT, yr * TOK + (s + 1) * SLOT)
                keys[dst, :] = piece[src, :DIM]
                values[dst, :] = piece[src, DIM:]

    for t in range(ALL // TILE):
        keys_t[t] = keys[t * TILE : (t + 1) * TILE, :].T
    key_acc[...] = jnp.zeros_like(key_acc)
    value_acc[...] = jnp.zeros_like(value_acc)
    query_acc[...] = jnp.zeros_like(query_acc)
    tops[...] = jnp.full_like(tops, LOW)
    sums[...] = jnp.zeros_like(sums)

    lane = lax.broadcasted_iota(jnp.int32, (1, ROWS), 1) & (SLOT - 1)
    for load in loads:
        load.wait()
    for i in range(BLOCKS):
        for c in range(ROWS // DIM):
            at = 2 * ROWS + ((i % 2) * (ROWS // DIM) + c) * (EXTRA // 2)
            coded = g_rows[i // 2, at : at + EXTRA // 2, :].astype(jnp.float32)
            d_rows[i : i + 1, c * DIM : (c + 1) * DIM] = coded[0:1] + coded[1:2] + coded[2:3]

    def place_of(v):
        i = plan[VISIT_BLOCK + v]
        return i, i // 2, pl.ds(pl.multiple_of(lax.rem(i, 2) * ROWS, ROWS), ROWS)

    def score_step(n, carry):
        raw = []
        for u in range(PACE):
            v = n * PACE + u
            i, yr, own = place_of(v)
            t = plan[VISIT_TILE + v]
            kt = keys[pl.ds(pl.multiple_of(t * TILE, TILE), TILE), :]
            raw.append(dot(kt, q_rows[yr, own, :], NT))
        for u, st in enumerate(raw):
            v = n * PACE + u
            i, slot = plan[VISIT_BLOCK + v], plan[VISIT_SLOT + v]
            k_pos = plan[VISIT_TILE + v] * TILE + lax.broadcasted_iota(jnp.int32, (TILE, ROWS), 0)
            q_pos = plan[VISIT_FIRST + v] + lane
            st = jnp.where((k_pos <= q_pos) & (k_pos >= starts[pl.ds(i, 1), :]), st, LOW)
            top = jnp.max(st, axis=0, keepdims=True)
            e = jnp.exp2((st - top) * (SCALE * LOG2E))
            scores[v] = e
            tops[slot, pl.ds(i, 1), :] = top
            sums[slot, pl.ds(i, 1), :] = jnp.sum(e, axis=0, keepdims=True)
        return carry

    steps = (plan[VISITS] + PACE - 1) // PACE
    lax.fori_loop(0, steps, score_step, 0)

    found = tops[:MAX_TILES]
    weights = jnp.exp2((found - jnp.max(found, axis=0, keepdims=True)) * (SCALE * LOG2E))
    total = jnp.sum(weights * sums[:MAX_TILES], axis=0, keepdims=True)
    tops[:MAX_TILES] = weights * (1.0 / total)
    tops[MAX_TILES] = jnp.zeros((BLOCKS, ROWS), jnp.float32)

    def grad_step(n, carry):
        low_pairs = []
        for u in range(PACE):
            v = n * PACE + u
            i, yr, own = place_of(v)
            rows = pl.ds(pl.multiple_of(plan[VISIT_TILE + v] * TILE, TILE), TILE)
            dprob = dot(values[rows, :], g_rows[yr, own, :], NT)
            prob = scores[v] * tops[plan[VISIT_SLOT + v], pl.ds(i, 1), :]
            dscore = prob * (dprob - d_rows[pl.ds(i, 1), :])
            low_pairs.append((prob.astype(jnp.bfloat16), dscore.astype(jnp.bfloat16)))
        terms = []
        for u, (prob, dscore) in enumerate(low_pairs):
            v = n * PACE + u
            i, yr, own = place_of(v)
            terms.append(
                (
                    dot(prob, g_rows[yr, own, :], NN),
                    dot(dscore, q_rows[yr, own, :], NN),
                    dot(keys_t[plan[VISIT_TILE + v]], dscore, NN),
                )
            )
        for u, (value_term, key_term, query_term) in enumerate(terms):
            v = n * PACE + u
            rows = pl.ds(pl.multiple_of(plan[VISIT_TILE + v] * TILE, TILE), TILE)
            value_acc[rows, :] += value_term
            key_acc[rows, :] += key_term
            query_acc[plan[VISIT_BLOCK + v]] += query_term
        return carry

    lax.fori_loop(0, steps, grad_step, 0)

    for i in range(BLOCKS):
        own = slice((i % 2) * ROWS, (i % 2 + 1) * ROWS)
        q_rows[i // 2, own, :] = (query_acc[i] * SCALE).astype(jnp.bfloat16).T

    stores = [
        pltpu.make_async_copy(q_rows.at[k], query_outs[k], sems.at[k]) for k in range(NY)
    ]
    for store in stores:
        store.start()
    for n, piece in enumerate(kv_outs):
        for yr in range(NY):
            for s in range(2):
                src = sorted_rows(n, yr, s)
                dst = slice(yr * TOK + s * SLOT, yr * TOK + (s + 1) * SLOT)
                piece[dst, :DIM] = (key_acc[src, :] * SCALE).astype(piece.dtype)
                piece[dst, DIM:] = value_acc[src, :].astype(piece.dtype)
    for store in stores:
        store.wait()


def attention_grads(plan, queries, grads, gathered):
    bf16, f32 = jnp.bfloat16, jnp.float32
    anywhere = pl.BlockSpec(memory_space=pl.ANY)
    return pl.pallas_call(
        main_body,
        out_shape=[jax.ShapeDtypeStruct((2 * ROWS, DIM), bf16)] * NY
        + [
            jax.ShapeDtypeStruct(
                (NY * TOK, 2 * DIM), bf16 if off in (NZ // 2 - 1, -(NZ // 2)) else f32
            )
            for off in OFFSETS
        ],
        in_specs=[scalars()] + whole(1) + [anywhere] * (2 * NY) + whole(NZ),
        out_specs=[anywhere] * NY + whole(NZ),
        scratch_shapes=[
            pltpu.VMEM((ALL, DIM), bf16),
            pltpu.VMEM((ALL, DIM), bf16),
            pltpu.VMEM((ALL // TILE, DIM, TILE), bf16),
            pltpu.VMEM((ALL, DIM), f32),
            pltpu.VMEM((ALL, DIM), f32),
            pltpu.VMEM((BLOCKS * MAX_TILES + PACE, TILE, ROWS), f32),
            pltpu.VMEM((MAX_TILES + 1, BLOCKS, ROWS), f32),
            pltpu.VMEM((MAX_TILES + 1, BLOCKS, ROWS), f32),
            pltpu.VMEM((BLOCKS, DIM, ROWS), f32),
            pltpu.VMEM((NY, 2 * ROWS, DIM), bf16),
            pltpu.VMEM((NY, GRAD_ROWS, DIM), bf16),
            pltpu.VMEM((BLOCKS, ROWS), f32),
            pltpu.SemaphoreType.DMA((2 * NY,)),
        ],
        compiler_params=params(40),
        name="attention_grads",
    )(*plan, *queries, *grads, *gathered)


def place_wide_body(*refs):
    y = own_y()
    for k in range(NY):
        start = lax.rem(y + k, NY) * WIDE
        for s in range(2):
            for h in range(GROUP):
                refs[NY][
                    s * SLOT : (s + 1) * SLOT,
                    pl.ds(pl.multiple_of(start + h * DIM, DIM), DIM),
                ] = refs[k][s * ROWS + h * SLOT : s * ROWS + (h + 1) * SLOT, :]


def place_wide(pieces):
    return pl.pallas_call(
        place_wide_body,
        out_shape=jax.ShapeDtypeStruct((TOK, HEADS * WIDE), jnp.bfloat16),
        in_specs=whole(NY),
        out_specs=pl.BlockSpec(memory_space=pltpu.VMEM),
        compiler_params=params(8),
        name="place_wide",
    )(*pieces)


def place_kv_body(*refs):
    y = own_y()
    for k in range(NY):
        refs[NY][:, column(y, k, DIM)] = refs[k][:, :DIM]
        refs[NY + 1][:, column(y, k, DIM)] = refs[k][:, DIM:]


def place_kv(pieces):
    return pl.pallas_call(
        place_kv_body,
        out_shape=[jax.ShapeDtypeStruct((TOK, HEADS * DIM), jnp.bfloat16)] * 2,
        in_specs=whole(NY),
        out_specs=whole(2),
        compiler_params=params(4),
        name="place_kv",
    )(*pieces)


def per_device(
    queries, key_projection, value_projection, forward_out, incoming, doc_lengths, pair_of
):
    def to_heads(pieces, move):
        return [pieces[0]] + [move(pieces[k], k) for k in range(1, NY)]

    with jax.named_scope("grads_shift"):
        out_grad = lax.ppermute(
            incoming[0], "pipe", [(p, (p - 1) % SECTIONS) for p in range(SECTIONS)]
        )
    with jax.named_scope("keys_values_in"):
        kv = to_heads(pack_kv(key_projection[0], value_projection[0]), along_y)
        packed_queries = pack_queries(queries[0])
        *kv, first, second, third, fourth = together(*kv, *packed_queries)
        packed_queries = [first, second, third, fourth]
        kv = jnp.concatenate(kv, axis=0)
    with jax.named_scope("queries_in"):
        query_pieces = to_heads(packed_queries, along_y)
    with jax.named_scope("plan"):
        plan = make_plan(pair_of, doc_lengths)
    with jax.named_scope("grads_pack"):
        out_grad, *query_pieces = together(out_grad, *query_pieces)
        packed_grads = pack_grads(out_grad, forward_out[0])
    with jax.named_scope("keys_values_ring"):
        gathered, plan, packed_grads = gather_z(kv, plan, packed_grads)
    with jax.named_scope("grads_in"):
        grad_pieces = to_heads(packed_grads, along_y)
    parts = attention_grads(plan, query_pieces, grad_pieces, gathered)
    query_parts, kv_parts = parts[:NY], parts[NY:]
    with jax.named_scope("query_grads_out"):
        query_parts = to_heads(query_parts, lambda x, k: along_y(x, -k))
    with jax.named_scope("key_value_grads_ring"):
        kv_sum, query_grad = sum_z(kv_parts, query_parts)
    with jax.named_scope("key_value_grads_out"):
        kv_pieces = [kv_sum[k * TOK : (k + 1) * TOK] for k in range(NY)]
        key_gradient, value_gradient = place_kv(
            to_heads(kv_pieces, lambda x, k: along_y(x, -k))
        )
    return query_grad[None], key_gradient[None], value_gradient[None]


def solution(mesh):
    tokens = P("pipe", "ctx", None)
    return jax.shard_map(
        per_device,
        mesh=mesh,
        in_specs=(tokens,) * 5 + (P("pipe", None),) * 2,
        out_specs=(tokens,) * 3,
        check_vma=False,
    )
```

```python
import functools
import math

import jax
import jax.numpy as jnp
from jax import lax
from jax.experimental import pallas as pl
from jax.experimental.pallas import tpu as pltpu
from jax.sharding import PartitionSpec as P

HEADS = 4
GROUP = 8
DIM = 128
TOK = 128
SLOT = 64
ROWS = GROUP * SLOT
DOCS = 16
NY = 4
NZ = 8
SECTIONS = 8
ALL = TOK * NY * NZ
BLOCKS = 2 * NY
TILE = 256
PACE = 4
PACK_STEP = 1
QUERY_STEP = 2
BACK_STEP = 3
WINDOW = 1024
MAX_TILES = 5
MAX_VISITS = 48
VISITS = 64
VISIT_BLOCK = 80
VISIT_TILE = VISIT_BLOCK + MAX_VISITS
VISIT_SLOT = VISIT_TILE + MAX_VISITS
VISIT_FIRST = VISIT_SLOT + MAX_VISITS
PLAN_SIZE = VISIT_FIRST + MAX_VISITS
SCALE = 1.0 / math.sqrt(DIM)
LOG2E = 1.4426950408889634
LOW = -1e30
WIDE = GROUP * DIM
EXTRA = 32
GRAD_ROWS = 2 * ROWS + 2 * (ROWS // DIM) * (EXTRA // 2)
OFFSETS = tuple(range(-(NZ // 2), NZ // 2))

NT = (((1,), (1,)), ((), ()))
NN = (((1,), (0,)), ((), ()))


def along_y(x, by):
    return lax.ppermute(
        x, "ctx", [(c, (c // NZ + by) % NY * NZ + c % NZ) for c in range(NY * NZ)]
    )


def along_z(x, by):
    return lax.ppermute(
        x, "ctx", [(c, c // NZ * NZ + (c % NZ + by) % NZ) for c in range(NY * NZ)]
    )


def together(*arrays):
    return lax.optimization_barrier(arrays)


def gather_z(x, query_pieces, packed):
    right = left = x
    pieces = {0: x}
    for step in range(1, NZ // 2):
        right, left = along_z(right, 1), along_z(left, -1)
        if step == PACK_STEP:
            right, left, *packed = together(right, left, *packed)
        if step == QUERY_STEP:
            right, left, *query_pieces = together(right, left, *query_pieces)
        if step not in (PACK_STEP, QUERY_STEP):
            right, left = together(right, left)
        pieces[-step], pieces[step] = right, left
    pieces[-(NZ // 2)] = along_z(right, 1)
    return [pieces[off] for off in OFFSETS], query_pieces, packed


def add_low(moving, own):
    return (moving.astype(jnp.float32) + own).astype(jnp.bfloat16)


def sum_z(parts, queries):
    parts = dict(zip(OFFSETS, parts))
    half = NZ // 2
    left, right = parts[-half], parts[half - 1]
    for step in range(1, half + 1):
        left = along_z(left, -1)
        if step < half:
            right = along_z(right, 1)
            if step == BACK_STEP:
                left, right, *queries = together(left, right, *queries)
            else:
                left, right = together(left, right)
            left = add_low(left, parts[step - half])
            if step < half - 1:
                right = add_low(right, parts[half - 1 - step])
    query_grad = place_wide(queries)
    left, query_grad = together(left, query_grad)
    total = parts[0] + left.astype(jnp.float32) + right.astype(jnp.float32)
    return total.astype(jnp.bfloat16), query_grad


def dot(a, b, dims):
    return lax.dot_general(a, b, dims, preferred_element_type=jnp.float32)


def whole(count):
    return [pl.BlockSpec(memory_space=pltpu.VMEM)] * count


def scalars():
    return pl.BlockSpec(memory_space=pltpu.SMEM)


def params(mib):
    return pltpu.CompilerParams(vmem_limit_bytes=mib << 20)


def own_y():
    return lax.axis_index("ctx") // NZ


def column(y, k, width):
    return pl.ds(pl.multiple_of(lax.rem(y + k, NY) * width, width), width)


def pack_kv_body(key, value, *outs):
    y = own_y()
    for k in range(NY):
        outs[k][:, :DIM] = key[:, column(y, k, DIM)]
        outs[k][:, DIM:] = value[:, column(y, k, DIM)]


def pack_kv(key, value):
    return pl.pallas_call(
        pack_kv_body,
        out_shape=[jax.ShapeDtypeStruct((TOK, 2 * DIM), jnp.bfloat16)] * NY,
        in_specs=whole(2),
        out_specs=whole(NY),
        compiler_params=params(4),
        name="pack_kv",
    )(key, value)


def stacked(piece, s):
    rows = slice(s * SLOT, (s + 1) * SLOT)
    return jnp.concatenate([piece[rows, h * DIM : (h + 1) * DIM] for h in range(GROUP)], axis=0)


def pack_queries_body(x, *outs):
    y = own_y()
    for k in range(NY):
        piece = x[:, column(y, k, WIDE)]
        for s in range(2):
            outs[k][s * ROWS : (s + 1) * ROWS, :] = stacked(piece, s)


def pack_queries(x):
    return pl.pallas_call(
        pack_queries_body,
        out_shape=[jax.ShapeDtypeStruct((2 * ROWS, DIM), jnp.bfloat16)] * NY,
        in_specs=whole(1),
        out_specs=whole(NY),
        compiler_params=params(8),
        name="pack_queries",
    )(x)


def pack_grads_body(grad, out, *outs):
    y = own_y()
    ones = jnp.ones((EXTRA // 2, DIM), jnp.bfloat16)
    line = lax.broadcasted_iota(jnp.int32, (EXTRA // 2, DIM), 0)
    for k in range(NY):
        columns = column(y, k, WIDE)
        piece = grad[:, columns]
        product = piece.astype(jnp.float32) * out[:, columns].astype(jnp.float32)
        high = product.astype(jnp.bfloat16)
        low = (product - high.astype(jnp.float32)).astype(jnp.bfloat16)
        for s in range(2):
            outs[k][s * ROWS : (s + 1) * ROWS, :] = stacked(piece, s)
            delta = dot(ones, stacked(high, s), NT) + dot(ones, stacked(low, s), NT)
            for c in range(ROWS // DIM):
                part = delta[:, c * DIM : (c + 1) * DIM]
                first = part.astype(jnp.bfloat16).astype(jnp.float32)
                second = (part - first).astype(jnp.bfloat16).astype(jnp.float32)
                third = part - first - second
                coded = jnp.where(line == 0, first, jnp.where(line == 1, second, third))
                at = 2 * ROWS + (s * (ROWS // DIM) + c) * (EXTRA // 2)
                outs[k][at : at + EXTRA // 2, :] = coded.astype(jnp.bfloat16)


def pack_grads(grad, out):
    return pl.pallas_call(
        pack_grads_body,
        out_shape=[jax.ShapeDtypeStruct((GRAD_ROWS, DIM), jnp.bfloat16)] * NY,
        in_specs=whole(2),
        out_specs=whole(NY),
        compiler_params=params(16),
        name="pack_grads",
    )(grad, out)


def plan_body(pairs, lengths, plan, starts):
    own = lax.axis_index("ctx")
    y, z = own // NZ, lax.rem(own, NZ)

    def block_at(zi, yr, s):
        pid = pairs[0, lax.rem(y + NY - yr, NY) * NZ + zi]
        return pid if s == 0 else 2 * NY * NZ - 1 - pid

    for n, off in enumerate(OFFSETS):
        for yr in range(NY):
            for s in range(2):
                plan[(n * NY + yr) * 2 + s] = block_at(lax.rem(z + NZ + off, NZ), yr, s) * SLOT

    ends = []
    for i in range(DOCS):
        ends.append(lengths[0, i] + (ends[-1] if ends else 0))

    def start_of(pos):
        start = jnp.zeros_like(pos)
        for end in ends:
            start = jnp.where(end <= pos, end, start)
        return start

    lane = lax.broadcasted_iota(jnp.int32, (BLOCKS, ROWS), 1) & (SLOT - 1)
    line = lax.broadcasted_iota(jnp.int32, (BLOCKS, ROWS), 0)
    firsts = jnp.zeros((BLOCKS, ROWS), jnp.int32)
    count = jnp.int32(0)
    for i in range(BLOCKS):
        first = block_at(z, i // 2, i % 2) * SLOT
        firsts = jnp.where(line == i, first, firsts)
        low_tile = start_of(first) // TILE
        high_tile = (first + SLOT - 1) // TILE + 1

        def list_tile(t, n, i=i, first=first, low_tile=low_tile):
            plan[VISIT_BLOCK + n] = i
            plan[VISIT_TILE + n] = t
            plan[VISIT_SLOT + n] = t - low_tile
            plan[VISIT_FIRST + n] = first
            return n + 1

        count = lax.fori_loop(low_tile, high_tile, list_tile, count)
    for extra in range(PACE - 1):
        plan[VISIT_BLOCK + count + extra] = 0
        plan[VISIT_TILE + count + extra] = 0
        plan[VISIT_SLOT + count + extra] = MAX_TILES
        plan[VISIT_FIRST + count + extra] = 0
    plan[VISITS] = count
    starts[...] = start_of(firsts + lane)


def make_plan(pairs, lengths):
    return pl.pallas_call(
        plan_body,
        out_shape=[
            jax.ShapeDtypeStruct((PLAN_SIZE,), jnp.int32),
            jax.ShapeDtypeStruct((BLOCKS, ROWS), jnp.int32),
        ],
        in_specs=[scalars(), scalars()],
        out_specs=[scalars(), pl.BlockSpec(memory_space=pltpu.VMEM)],
        compiler_params=params(4),
        name="make_plan",
    )(pairs, lengths)


def main_body(plan, starts, *refs):
    queries, grads, gathered = refs[0:NY], refs[NY : 2 * NY], refs[2 * NY : 2 * NY + NZ]
    query_outs = refs[2 * NY + NZ : 3 * NY + NZ]
    kv_outs = refs[3 * NY + NZ : 3 * NY + 2 * NZ]
    keys, values, keys_t, key_acc, value_acc, scores, tops, sums, query_acc = refs[
        3 * NY + 2 * NZ : 3 * NY + 2 * NZ + 9
    ]
    q_rows, g_rows, d_rows, sems = refs[3 * NY + 2 * NZ + 9 :]

    loads = [pltpu.make_async_copy(queries[k], q_rows.at[k], sems.at[k]) for k in range(NY)]
    loads += [pltpu.make_async_copy(grads[k], g_rows.at[k], sems.at[NY + k]) for k in range(NY)]
    for load in loads:
        load.start()

    def sorted_rows(n, yr, s):
        return pl.ds(pl.multiple_of(plan[(n * NY + yr) * 2 + s], SLOT), SLOT)

    for n, piece in enumerate(gathered):
        for yr in range(NY):
            for s in range(2):
                dst = sorted_rows(n, yr, s)
                src = slice(yr * TOK + s * SLOT, yr * TOK + (s + 1) * SLOT)
                keys[dst, :] = piece[src, :DIM]
                values[dst, :] = piece[src, DIM:]

    for t in range(ALL // TILE):
        keys_t[t] = keys[t * TILE : (t + 1) * TILE, :].T
    key_acc[...] = jnp.zeros_like(key_acc)
    value_acc[...] = jnp.zeros_like(value_acc)
    query_acc[...] = jnp.zeros_like(query_acc)
    tops[...] = jnp.full_like(tops, LOW)
    sums[...] = jnp.zeros_like(sums)

    lane = lax.broadcasted_iota(jnp.int32, (1, ROWS), 1) & (SLOT - 1)
    for load in loads:
        load.wait()
    for i in range(BLOCKS):
        for c in range(ROWS // DIM):
            at = 2 * ROWS + ((i % 2) * (ROWS // DIM) + c) * (EXTRA // 2)
            coded = g_rows[i // 2, at : at + EXTRA // 2, :].astype(jnp.float32)
            d_rows[i : i + 1, c * DIM : (c + 1) * DIM] = coded[0:1] + coded[1:2] + coded[2:3]

    def place_of(v):
        i = plan[VISIT_BLOCK + v]
        return i, i // 2, pl.ds(pl.multiple_of(lax.rem(i, 2) * ROWS, ROWS), ROWS)

    def score_step(n, carry):
        raw = []
        for u in range(PACE):
            v = n * PACE + u
            i, yr, own = place_of(v)
            t = plan[VISIT_TILE + v]
            kt = keys[pl.ds(pl.multiple_of(t * TILE, TILE), TILE), :]
            raw.append(dot(kt, q_rows[yr, own, :], NT))
        for u, st in enumerate(raw):
            v = n * PACE + u
            i, slot = plan[VISIT_BLOCK + v], plan[VISIT_SLOT + v]
            k_pos = plan[VISIT_TILE + v] * TILE + lax.broadcasted_iota(jnp.int32, (TILE, ROWS), 0)
            q_pos = plan[VISIT_FIRST + v] + lane
            st = jnp.where((k_pos <= q_pos) & (k_pos >= starts[pl.ds(i, 1), :]), st, LOW)
            top = jnp.max(st, axis=0, keepdims=True)
            e = jnp.exp2((st - top) * (SCALE * LOG2E))
            scores[v] = e
            tops[slot, pl.ds(i, 1), :] = top
            sums[slot, pl.ds(i, 1), :] = jnp.sum(e, axis=0, keepdims=True)
        return carry

    steps = (plan[VISITS] + PACE - 1) // PACE
    lax.fori_loop(0, steps, score_step, 0)

    found = tops[:MAX_TILES]
    weights = jnp.exp2((found - jnp.max(found, axis=0, keepdims=True)) * (SCALE * LOG2E))
    total = jnp.sum(weights * sums[:MAX_TILES], axis=0, keepdims=True)
    tops[:MAX_TILES] = weights * (1.0 / total)
    tops[MAX_TILES] = jnp.zeros((BLOCKS, ROWS), jnp.float32)

    def grad_step(n, carry):
        low_pairs = []
        for u in range(PACE):
            v = n * PACE + u
            i, yr, own = place_of(v)
            rows = pl.ds(pl.multiple_of(plan[VISIT_TILE + v] * TILE, TILE), TILE)
            dprob = dot(values[rows, :], g_rows[yr, own, :], NT)
            prob = scores[v] * tops[plan[VISIT_SLOT + v], pl.ds(i, 1), :]
            dscore = prob * (dprob - d_rows[pl.ds(i, 1), :])
            low_pairs.append((prob.astype(jnp.bfloat16), dscore.astype(jnp.bfloat16)))
        terms = []
        for u, (prob, dscore) in enumerate(low_pairs):
            v = n * PACE + u
            i, yr, own = place_of(v)
            terms.append(
                (
                    dot(prob, g_rows[yr, own, :], NN),
                    dot(dscore, q_rows[yr, own, :], NN),
                    dot(keys_t[plan[VISIT_TILE + v]], dscore, NN),
                )
            )
        for u, (value_term, key_term, query_term) in enumerate(terms):
            v = n * PACE + u
            rows = pl.ds(pl.multiple_of(plan[VISIT_TILE + v] * TILE, TILE), TILE)
            value_acc[rows, :] += value_term
            key_acc[rows, :] += key_term
            query_acc[plan[VISIT_BLOCK + v]] += query_term
        return carry

    lax.fori_loop(0, steps, grad_step, 0)

    for i in range(BLOCKS):
        own = slice((i % 2) * ROWS, (i % 2 + 1) * ROWS)
        q_rows[i // 2, own, :] = (query_acc[i] * SCALE).astype(jnp.bfloat16).T

    stores = [
        pltpu.make_async_copy(q_rows.at[k], query_outs[k], sems.at[k]) for k in range(NY)
    ]
    for store in stores:
        store.start()
    for n, piece in enumerate(kv_outs):
        for yr in range(NY):
            for s in range(2):
                src = sorted_rows(n, yr, s)
                dst = slice(yr * TOK + s * SLOT, yr * TOK + (s + 1) * SLOT)
                piece[dst, :DIM] = (key_acc[src, :] * SCALE).astype(piece.dtype)
                piece[dst, DIM:] = value_acc[src, :].astype(piece.dtype)
    for store in stores:
        store.wait()


def attention_grads(plan, queries, grads, gathered):
    bf16, f32 = jnp.bfloat16, jnp.float32
    anywhere = pl.BlockSpec(memory_space=pl.ANY)
    return pl.pallas_call(
        main_body,
        out_shape=[jax.ShapeDtypeStruct((2 * ROWS, DIM), bf16)] * NY
        + [
            jax.ShapeDtypeStruct(
                (NY * TOK, 2 * DIM), bf16 if off in (NZ // 2 - 1, -(NZ // 2)) else f32
            )
            for off in OFFSETS
        ],
        in_specs=[scalars()] + whole(1) + [anywhere] * (2 * NY) + whole(NZ),
        out_specs=[anywhere] * NY + whole(NZ),
        scratch_shapes=[
            pltpu.VMEM((ALL, DIM), bf16),
            pltpu.VMEM((ALL, DIM), bf16),
            pltpu.VMEM((ALL // TILE, DIM, TILE), bf16),
            pltpu.VMEM((ALL, DIM), f32),
            pltpu.VMEM((ALL, DIM), f32),
            pltpu.VMEM((BLOCKS * MAX_TILES + PACE, TILE, ROWS), f32),
            pltpu.VMEM((MAX_TILES + 1, BLOCKS, ROWS), f32),
            pltpu.VMEM((MAX_TILES + 1, BLOCKS, ROWS), f32),
            pltpu.VMEM((BLOCKS, DIM, ROWS), f32),
            pltpu.VMEM((NY, 2 * ROWS, DIM), bf16),
            pltpu.VMEM((NY, GRAD_ROWS, DIM), bf16),
            pltpu.VMEM((BLOCKS, ROWS), f32),
            pltpu.SemaphoreType.DMA((2 * NY,)),
        ],
        compiler_params=params(40),
        name="attention_grads",
    )(*plan, *queries, *grads, *gathered)


def place_wide_body(*refs):
    y = own_y()
    for k in range(NY):
        start = lax.rem(y + k, NY) * WIDE
        for s in range(2):
            for h in range(GROUP):
                refs[NY][
                    s * SLOT : (s + 1) * SLOT,
                    pl.ds(pl.multiple_of(start + h * DIM, DIM), DIM),
                ] = refs[k][s * ROWS + h * SLOT : s * ROWS + (h + 1) * SLOT, :]


def place_wide(pieces):
    return pl.pallas_call(
        place_wide_body,
        out_shape=jax.ShapeDtypeStruct((TOK, HEADS * WIDE), jnp.bfloat16),
        in_specs=whole(NY),
        out_specs=pl.BlockSpec(memory_space=pltpu.VMEM),
        compiler_params=params(8),
        name="place_wide",
    )(*pieces)


def place_kv_body(*refs):
    y = own_y()
    for k in range(NY):
        refs[NY][:, column(y, k, DIM)] = refs[k][:, :DIM]
        refs[NY + 1][:, column(y, k, DIM)] = refs[k][:, DIM:]


def place_kv(pieces):
    return pl.pallas_call(
        place_kv_body,
        out_shape=[jax.ShapeDtypeStruct((TOK, HEADS * DIM), jnp.bfloat16)] * 2,
        in_specs=whole(NY),
        out_specs=whole(2),
        compiler_params=params(4),
        name="place_kv",
    )(*pieces)


def per_device(
    queries, key_projection, value_projection, forward_out, incoming, doc_lengths, pair_of
):
    def to_heads(pieces, move):
        return [pieces[0]] + [move(pieces[k], k) for k in range(1, NY)]

    with jax.named_scope("grads_shift"):
        out_grad = lax.ppermute(
            incoming[0], "pipe", [(p, (p - 1) % SECTIONS) for p in range(SECTIONS)]
        )
    with jax.named_scope("keys_values_in"):
        kv = to_heads(pack_kv(key_projection[0], value_projection[0]), along_y)
        packed_queries = pack_queries(queries[0])
        *kv, first, second, third, fourth = together(*kv, *packed_queries)
        packed_queries = [first, second, third, fourth]
        kv = jnp.concatenate(kv, axis=0)
    with jax.named_scope("queries_in"):
        query_pieces = to_heads(packed_queries, along_y)
    with jax.named_scope("plan"):
        plan = make_plan(pair_of, doc_lengths)
    with jax.named_scope("grads_pack"):
        packed_grads = pack_grads(out_grad, forward_out[0])
    with jax.named_scope("keys_values_ring"):
        gathered, query_pieces, packed = gather_z(kv, query_pieces, [*plan, *packed_grads])
        plan, packed_grads = packed[:2], packed[2:]
    with jax.named_scope("grads_in"):
        grad_pieces = to_heads(packed_grads, along_y)
    parts = attention_grads(plan, query_pieces, grad_pieces, gathered)
    query_parts, kv_parts = parts[:NY], parts[NY:]
    with jax.named_scope("query_grads_out"):
        query_parts = to_heads(query_parts, lambda x, k: along_y(x, -k))
    with jax.named_scope("key_value_grads_ring"):
        kv_sum, query_grad = sum_z(kv_parts, query_parts)
    with jax.named_scope("key_value_grads_out"):
        kv_pieces = [kv_sum[k * TOK : (k + 1) * TOK] for k in range(NY)]
        key_gradient, value_gradient = place_kv(
            to_heads(kv_pieces, lambda x, k: along_y(x, -k))
        )
    return query_grad[None], key_gradient[None], value_gradient[None]


def solution(mesh):
    tokens = P("pipe", "ctx", None)
    return jax.shard_map(
        per_device,
        mesh=mesh,
        in_specs=(tokens,) * 5 + (P("pipe", None),) * 2,
        out_specs=(tokens,) * 3,
        check_vma=False,
    )
```

```python
import functools
import math

import jax
import jax.numpy as jnp
from jax import lax
from jax.experimental import pallas as pl
from jax.experimental.pallas import tpu as pltpu
from jax.sharding import PartitionSpec as P

HEADS = 4
GROUP = 8
DIM = 128
TOK = 128
SLOT = 64
ROWS = GROUP * SLOT
DOCS = 16
NY = 4
NZ = 8
SECTIONS = 8
ALL = TOK * NY * NZ
BLOCKS = 2 * NY
TILE = 256
PACE = 4
PACK_STEP = 1
QUERY_STEP = 2
BACK_STEP = 2
WINDOW = 1024
MAX_TILES = 5
MAX_VISITS = 48
VISITS = 64
VISIT_BLOCK = 80
VISIT_TILE = VISIT_BLOCK + MAX_VISITS
VISIT_SLOT = VISIT_TILE + MAX_VISITS
VISIT_FIRST = VISIT_SLOT + MAX_VISITS
PLAN_SIZE = VISIT_FIRST + MAX_VISITS
SCALE = 1.0 / math.sqrt(DIM)
LOG2E = 1.4426950408889634
LOW = -1e30
WIDE = GROUP * DIM
EXTRA = 32
GRAD_ROWS = 2 * ROWS + 2 * (ROWS // DIM) * (EXTRA // 2)
OFFSETS = tuple(range(-(NZ // 2), NZ // 2))

NT = (((1,), (1,)), ((), ()))
NN = (((1,), (0,)), ((), ()))


def along_y(x, by):
    return lax.ppermute(
        x, "ctx", [(c, (c // NZ + by) % NY * NZ + c % NZ) for c in range(NY * NZ)]
    )


def along_z(x, by):
    return lax.ppermute(
        x, "ctx", [(c, c // NZ * NZ + (c % NZ + by) % NZ) for c in range(NY * NZ)]
    )


def together(*arrays):
    return lax.optimization_barrier(arrays)


def gather_z(x, query_pieces, packed):
    right = left = x
    pieces = {0: x}
    for step in range(1, NZ // 2):
        right, left = along_z(right, 1), along_z(left, -1)
        if step == PACK_STEP:
            right, left, *packed = together(right, left, *packed)
        if step == QUERY_STEP:
            right, left, *query_pieces = together(right, left, *query_pieces)
        if step not in (PACK_STEP, QUERY_STEP):
            right, left = together(right, left)
        pieces[-step], pieces[step] = right, left
    pieces[-(NZ // 2)] = along_z(right, 1)
    return [pieces[off] for off in OFFSETS], query_pieces, packed


def add_low(moving, own):
    return (moving.astype(jnp.float32) + own).astype(jnp.bfloat16)


def sum_z(parts, queries):
    parts = dict(zip(OFFSETS, parts))
    half = NZ // 2
    left, right = parts[-half], parts[half - 1]
    for step in range(1, half + 1):
        left = along_z(left, -1)
        if step < half:
            right = along_z(right, 1)
            if step == BACK_STEP:
                left, right, *queries = together(left, right, *queries)
            else:
                left, right = together(left, right)
            left = add_low(left, parts[step - half])
            if step < half - 1:
                right = add_low(right, parts[half - 1 - step])
    query_grad = place_wide(queries)
    left, query_grad = together(left, query_grad)
    total = parts[0] + left.astype(jnp.float32) + right.astype(jnp.float32)
    return total.astype(jnp.bfloat16), query_grad


def dot(a, b, dims):
    return lax.dot_general(a, b, dims, preferred_element_type=jnp.float32)


def whole(count):
    return [pl.BlockSpec(memory_space=pltpu.VMEM)] * count


def scalars():
    return pl.BlockSpec(memory_space=pltpu.SMEM)


def params(mib):
    return pltpu.CompilerParams(vmem_limit_bytes=mib << 20)


def own_y():
    return lax.axis_index("ctx") // NZ


def column(y, k, width):
    return pl.ds(pl.multiple_of(lax.rem(y + k, NY) * width, width), width)


def pack_kv_body(key, value, *outs):
    y = own_y()
    for k in range(NY):
        outs[k][:, :DIM] = key[:, column(y, k, DIM)]
        outs[k][:, DIM:] = value[:, column(y, k, DIM)]


def pack_kv(key, value):
    return pl.pallas_call(
        pack_kv_body,
        out_shape=[jax.ShapeDtypeStruct((TOK, 2 * DIM), jnp.bfloat16)] * NY,
        in_specs=whole(2),
        out_specs=whole(NY),
        compiler_params=params(4),
        name="pack_kv",
    )(key, value)


def stacked(piece, s):
    rows = slice(s * SLOT, (s + 1) * SLOT)
    return jnp.concatenate([piece[rows, h * DIM : (h + 1) * DIM] for h in range(GROUP)], axis=0)


def pack_queries_body(x, *outs):
    y = own_y()
    for k in range(NY):
        piece = x[:, column(y, k, WIDE)]
        for s in range(2):
            outs[k][s * ROWS : (s + 1) * ROWS, :] = stacked(piece, s)


def pack_queries(x):
    return pl.pallas_call(
        pack_queries_body,
        out_shape=[jax.ShapeDtypeStruct((2 * ROWS, DIM), jnp.bfloat16)] * NY,
        in_specs=whole(1),
        out_specs=whole(NY),
        compiler_params=params(8),
        name="pack_queries",
    )(x)


def pack_grads_body(grad, out, *outs):
    y = own_y()
    ones = jnp.ones((EXTRA // 2, DIM), jnp.bfloat16)
    line = lax.broadcasted_iota(jnp.int32, (EXTRA // 2, DIM), 0)
    for k in range(NY):
        columns = column(y, k, WIDE)
        piece = grad[:, columns]
        product = piece.astype(jnp.float32) * out[:, columns].astype(jnp.float32)
        high = product.astype(jnp.bfloat16)
        low = (product - high.astype(jnp.float32)).astype(jnp.bfloat16)
        for s in range(2):
            outs[k][s * ROWS : (s + 1) * ROWS, :] = stacked(piece, s)
            delta = dot(ones, stacked(high, s), NT) + dot(ones, stacked(low, s), NT)
            for c in range(ROWS // DIM):
                part = delta[:, c * DIM : (c + 1) * DIM]
                first = part.astype(jnp.bfloat16).astype(jnp.float32)
                second = (part - first).astype(jnp.bfloat16).astype(jnp.float32)
                third = part - first - second
                coded = jnp.where(line == 0, first, jnp.where(line == 1, second, third))
                at = 2 * ROWS + (s * (ROWS // DIM) + c) * (EXTRA // 2)
                outs[k][at : at + EXTRA // 2, :] = coded.astype(jnp.bfloat16)


def pack_grads(grad, out):
    return pl.pallas_call(
        pack_grads_body,
        out_shape=[jax.ShapeDtypeStruct((GRAD_ROWS, DIM), jnp.bfloat16)] * NY,
        in_specs=whole(2),
        out_specs=whole(NY),
        compiler_params=params(16),
        name="pack_grads",
    )(grad, out)


def plan_body(pairs, lengths, plan, starts):
    own = lax.axis_index("ctx")
    y, z = own // NZ, lax.rem(own, NZ)

    def block_at(zi, yr, s):
        pid = pairs[0, lax.rem(y + NY - yr, NY) * NZ + zi]
        return pid if s == 0 else 2 * NY * NZ - 1 - pid

    for n, off in enumerate(OFFSETS):
        for yr in range(NY):
            for s in range(2):
                plan[(n * NY + yr) * 2 + s] = block_at(lax.rem(z + NZ + off, NZ), yr, s) * SLOT

    ends = []
    for i in range(DOCS):
        ends.append(lengths[0, i] + (ends[-1] if ends else 0))

    def start_of(pos):
        start = jnp.zeros_like(pos)
        for end in ends:
            start = jnp.where(end <= pos, end, start)
        return start

    lane = lax.broadcasted_iota(jnp.int32, (BLOCKS, ROWS), 1) & (SLOT - 1)
    line = lax.broadcasted_iota(jnp.int32, (BLOCKS, ROWS), 0)
    firsts = jnp.zeros((BLOCKS, ROWS), jnp.int32)
    count = jnp.int32(0)
    for i in range(BLOCKS):
        first = block_at(z, i // 2, i % 2) * SLOT
        firsts = jnp.where(line == i, first, firsts)
        low_tile = start_of(first) // TILE
        high_tile = (first + SLOT - 1) // TILE + 1

        def list_tile(t, n, i=i, first=first, low_tile=low_tile):
            plan[VISIT_BLOCK + n] = i
            plan[VISIT_TILE + n] = t
            plan[VISIT_SLOT + n] = t - low_tile
            plan[VISIT_FIRST + n] = first
            return n + 1

        count = lax.fori_loop(low_tile, high_tile, list_tile, count)
    for extra in range(PACE - 1):
        plan[VISIT_BLOCK + count + extra] = 0
        plan[VISIT_TILE + count + extra] = 0
        plan[VISIT_SLOT + count + extra] = MAX_TILES
        plan[VISIT_FIRST + count + extra] = 0
    plan[VISITS] = count
    starts[...] = start_of(firsts + lane)


def make_plan(pairs, lengths):
    return pl.pallas_call(
        plan_body,
        out_shape=[
            jax.ShapeDtypeStruct((PLAN_SIZE,), jnp.int32),
            jax.ShapeDtypeStruct((BLOCKS, ROWS), jnp.int32),
        ],
        in_specs=[scalars(), scalars()],
        out_specs=[scalars(), pl.BlockSpec(memory_space=pltpu.VMEM)],
        compiler_params=params(4),
        name="make_plan",
    )(pairs, lengths)


def main_body(plan, starts, *refs):
    queries, grads, gathered = refs[0:NY], refs[NY : 2 * NY], refs[2 * NY : 2 * NY + NZ]
    query_outs = refs[2 * NY + NZ : 3 * NY + NZ]
    kv_outs = refs[3 * NY + NZ : 3 * NY + 2 * NZ]
    keys, values, keys_t, key_acc, value_acc, scores, tops, sums, query_acc = refs[
        3 * NY + 2 * NZ : 3 * NY + 2 * NZ + 9
    ]
    q_rows, g_rows, d_rows, sems = refs[3 * NY + 2 * NZ + 9 :]

    loads = [pltpu.make_async_copy(queries[k], q_rows.at[k], sems.at[k]) for k in range(NY)]
    loads += [pltpu.make_async_copy(grads[k], g_rows.at[k], sems.at[NY + k]) for k in range(NY)]
    for load in loads:
        load.start()

    def sorted_rows(n, yr, s):
        return pl.ds(pl.multiple_of(plan[(n * NY + yr) * 2 + s], SLOT), SLOT)

    for n, piece in enumerate(gathered):
        for yr in range(NY):
            for s in range(2):
                dst = sorted_rows(n, yr, s)
                src = slice(yr * TOK + s * SLOT, yr * TOK + (s + 1) * SLOT)
                keys[dst, :] = piece[src, :DIM]
                values[dst, :] = piece[src, DIM:]

    for t in range(ALL // TILE):
        keys_t[t] = keys[t * TILE : (t + 1) * TILE, :].T
    key_acc[...] = jnp.zeros_like(key_acc)
    value_acc[...] = jnp.zeros_like(value_acc)
    query_acc[...] = jnp.zeros_like(query_acc)
    tops[...] = jnp.full_like(tops, LOW)
    sums[...] = jnp.zeros_like(sums)

    lane = lax.broadcasted_iota(jnp.int32, (1, ROWS), 1) & (SLOT - 1)
    for load in loads:
        load.wait()
    for i in range(BLOCKS):
        for c in range(ROWS // DIM):
            at = 2 * ROWS + ((i % 2) * (ROWS // DIM) + c) * (EXTRA // 2)
            coded = g_rows[i // 2, at : at + EXTRA // 2, :].astype(jnp.float32)
            d_rows[i : i + 1, c * DIM : (c + 1) * DIM] = coded[0:1] + coded[1:2] + coded[2:3]

    def place_of(v):
        i = plan[VISIT_BLOCK + v]
        return i, i // 2, pl.ds(pl.multiple_of(lax.rem(i, 2) * ROWS, ROWS), ROWS)

    def score_step(n, carry):
        raw = []
        for u in range(PACE):
            v = n * PACE + u
            i, yr, own = place_of(v)
            t = plan[VISIT_TILE + v]
            kt = keys[pl.ds(pl.multiple_of(t * TILE, TILE), TILE), :]
            raw.append(dot(kt, q_rows[yr, own, :], NT))
        for u, st in enumerate(raw):
            v = n * PACE + u
            i, slot = plan[VISIT_BLOCK + v], plan[VISIT_SLOT + v]
            k_pos = plan[VISIT_TILE + v] * TILE + lax.broadcasted_iota(jnp.int32, (TILE, ROWS), 0)
            q_pos = plan[VISIT_FIRST + v] + lane
            st = jnp.where((k_pos <= q_pos) & (k_pos >= starts[pl.ds(i, 1), :]), st, LOW)
            top = jnp.max(st, axis=0, keepdims=True)
            e = jnp.exp2((st - top) * (SCALE * LOG2E))
            scores[v] = e
            tops[slot, pl.ds(i, 1), :] = top
            sums[slot, pl.ds(i, 1), :] = jnp.sum(e, axis=0, keepdims=True)
        return carry

    steps = (plan[VISITS] + PACE - 1) // PACE
    lax.fori_loop(0, steps, score_step, 0)

    found = tops[:MAX_TILES]
    weights = jnp.exp2((found - jnp.max(found, axis=0, keepdims=True)) * (SCALE * LOG2E))
    total = jnp.sum(weights * sums[:MAX_TILES], axis=0, keepdims=True)
    tops[:MAX_TILES] = weights * (1.0 / total)
    tops[MAX_TILES] = jnp.zeros((BLOCKS, ROWS), jnp.float32)

    def grad_step(n, carry):
        low_pairs = []
        for u in range(PACE):
            v = n * PACE + u
            i, yr, own = place_of(v)
            rows = pl.ds(pl.multiple_of(plan[VISIT_TILE + v] * TILE, TILE), TILE)
            dprob = dot(values[rows, :], g_rows[yr, own, :], NT)
            prob = scores[v] * tops[plan[VISIT_SLOT + v], pl.ds(i, 1), :]
            dscore = prob * (dprob - d_rows[pl.ds(i, 1), :])
            low_pairs.append((prob.astype(jnp.bfloat16), dscore.astype(jnp.bfloat16)))
        terms = []
        for u, (prob, dscore) in enumerate(low_pairs):
            v = n * PACE + u
            i, yr, own = place_of(v)
            terms.append(
                (
                    dot(prob, g_rows[yr, own, :], NN),
                    dot(dscore, q_rows[yr, own, :], NN),
                    dot(keys_t[plan[VISIT_TILE + v]], dscore, NN),
                )
            )
        for u, (value_term, key_term, query_term) in enumerate(terms):
            v = n * PACE + u
            rows = pl.ds(pl.multiple_of(plan[VISIT_TILE + v] * TILE, TILE), TILE)
            value_acc[rows, :] += value_term
            key_acc[rows, :] += key_term
            query_acc[plan[VISIT_BLOCK + v]] += query_term
        return carry

    lax.fori_loop(0, steps, grad_step, 0)

    for i in range(BLOCKS):
        own = slice((i % 2) * ROWS, (i % 2 + 1) * ROWS)
        q_rows[i // 2, own, :] = (query_acc[i] * SCALE).astype(jnp.bfloat16).T

    stores = [
        pltpu.make_async_copy(q_rows.at[k], query_outs[k], sems.at[k]) for k in range(NY)
    ]
    for store in stores:
        store.start()
    for n, piece in enumerate(kv_outs):
        for yr in range(NY):
            for s in range(2):
                src = sorted_rows(n, yr, s)
                dst = slice(yr * TOK + s * SLOT, yr * TOK + (s + 1) * SLOT)
                piece[dst, :DIM] = (key_acc[src, :] * SCALE).astype(piece.dtype)
                piece[dst, DIM:] = value_acc[src, :].astype(piece.dtype)
    for store in stores:
        store.wait()


def attention_grads(plan, queries, grads, gathered):
    bf16, f32 = jnp.bfloat16, jnp.float32
    anywhere = pl.BlockSpec(memory_space=pl.ANY)
    return pl.pallas_call(
        main_body,
        out_shape=[jax.ShapeDtypeStruct((2 * ROWS, DIM), bf16)] * NY
        + [
            jax.ShapeDtypeStruct(
                (NY * TOK, 2 * DIM), bf16 if off in (NZ // 2 - 1, -(NZ // 2)) else f32
            )
            for off in OFFSETS
        ],
        in_specs=[scalars()] + whole(1) + [anywhere] * (2 * NY) + whole(NZ),
        out_specs=[anywhere] * NY + whole(NZ),
        scratch_shapes=[
            pltpu.VMEM((ALL, DIM), bf16),
            pltpu.VMEM((ALL, DIM), bf16),
            pltpu.VMEM((ALL // TILE, DIM, TILE), bf16),
            pltpu.VMEM((ALL, DIM), f32),
            pltpu.VMEM((ALL, DIM), f32),
            pltpu.VMEM((BLOCKS * MAX_TILES + PACE, TILE, ROWS), f32),
            pltpu.VMEM((MAX_TILES + 1, BLOCKS, ROWS), f32),
            pltpu.VMEM((MAX_TILES + 1, BLOCKS, ROWS), f32),
            pltpu.VMEM((BLOCKS, DIM, ROWS), f32),
            pltpu.VMEM((NY, 2 * ROWS, DIM), bf16),
            pltpu.VMEM((NY, GRAD_ROWS, DIM), bf16),
            pltpu.VMEM((BLOCKS, ROWS), f32),
            pltpu.SemaphoreType.DMA((2 * NY,)),
        ],
        compiler_params=params(40),
        name="attention_grads",
    )(*plan, *queries, *grads, *gathered)


def place_wide_body(*refs):
    y = own_y()
    for k in range(NY):
        start = lax.rem(y + k, NY) * WIDE
        for s in range(2):
            for h in range(GROUP):
                refs[NY][
                    s * SLOT : (s + 1) * SLOT,
                    pl.ds(pl.multiple_of(start + h * DIM, DIM), DIM),
                ] = refs[k][s * ROWS + h * SLOT : s * ROWS + (h + 1) * SLOT, :]


def place_wide(pieces):
    return pl.pallas_call(
        place_wide_body,
        out_shape=jax.ShapeDtypeStruct((TOK, HEADS * WIDE), jnp.bfloat16),
        in_specs=whole(NY),
        out_specs=pl.BlockSpec(memory_space=pltpu.VMEM),
        compiler_params=params(8),
        name="place_wide",
    )(*pieces)


def place_kv_body(*refs):
    y = own_y()
    for k in range(NY):
        refs[NY][:, column(y, k, DIM)] = refs[k][:, :DIM]
        refs[NY + 1][:, column(y, k, DIM)] = refs[k][:, DIM:]


def place_kv(pieces):
    return pl.pallas_call(
        place_kv_body,
        out_shape=[jax.ShapeDtypeStruct((TOK, HEADS * DIM), jnp.bfloat16)] * 2,
        in_specs=whole(NY),
        out_specs=whole(2),
        compiler_params=params(4),
        name="place_kv",
    )(*pieces)


def per_device(
    queries, key_projection, value_projection, forward_out, incoming, doc_lengths, pair_of
):
    def to_heads(pieces, move):
        return [pieces[0]] + [move(pieces[k], k) for k in range(1, NY)]

    with jax.named_scope("grads_shift"):
        out_grad = lax.ppermute(
            incoming[0], "pipe", [(p, (p - 1) % SECTIONS) for p in range(SECTIONS)]
        )
    with jax.named_scope("keys_values_in"):
        kv = to_heads(pack_kv(key_projection[0], value_projection[0]), along_y)
        packed_queries = pack_queries(queries[0])
        *kv, first, second, third, fourth = together(*kv, *packed_queries)
        packed_queries = [first, second, third, fourth]
        kv = jnp.concatenate(kv, axis=0)
    with jax.named_scope("queries_in"):
        query_pieces = to_heads(packed_queries, along_y)
    with jax.named_scope("plan"):
        plan = make_plan(pair_of, doc_lengths)
    with jax.named_scope("grads_pack"):
        packed_grads = pack_grads(out_grad, forward_out[0])
    with jax.named_scope("keys_values_ring"):
        gathered, query_pieces, packed = gather_z(kv, query_pieces, [*plan, *packed_grads])
        plan, packed_grads = packed[:2], packed[2:]
    with jax.named_scope("grads_in"):
        grad_pieces = to_heads(packed_grads, along_y)
    parts = attention_grads(plan, query_pieces, grad_pieces, gathered)
    query_parts, kv_parts = parts[:NY], parts[NY:]
    with jax.named_scope("query_grads_out"):
        query_parts = to_heads(query_parts, lambda x, k: along_y(x, -k))
    with jax.named_scope("key_value_grads_ring"):
        kv_sum, query_grad = sum_z(kv_parts, query_parts)
    with jax.named_scope("key_value_grads_out"):
        kv_pieces = [kv_sum[k * TOK : (k + 1) * TOK] for k in range(NY)]
        key_gradient, value_gradient = place_kv(
            to_heads(kv_pieces, lambda x, k: along_y(x, -k))
        )
    return query_grad[None], key_gradient[None], value_gradient[None]


def solution(mesh):
    tokens = P("pipe", "ctx", None)
    return jax.shard_map(
        per_device,
        mesh=mesh,
        in_specs=(tokens,) * 5 + (P("pipe", None),) * 2,
        out_specs=(tokens,) * 3,
        check_vma=False,
    )
```
